128 devices in a mesh: row: 16 (over y, x), samp: 8 (over z, core).
Axes of the slice: x: 4, y: 4, z: 4, core: 2. Of those that a mesh axis runs over, the one named last changes fastest.
Arguments:
- fibres_first: float32 [16384, 16384], P('row', 'samp'), may hold values from -768 to 768
- fibres_second: float32 [16384, 16384], P('row', 'samp'), may hold values from -768 to 768
- index_first: int32 [16384, 2], P('samp'), may hold values from 0 to 16383, as said below
- index_second: int32 [16384, 2], P('samp'), may hold values from 0 to 16383, as said below
- factor_b: float32 [16384, 256], P('row'), may hold values from -6 to 6
- factor_c: float32 [16384, 256], P('row'), may hold values from -6 to 6
Outputs:
- factor_a: float32 [16384, 256], P('row')
- factor_b_new: float32 [16384, 256], P('row')
- weights: float32 [256], replicated
The draws below stay inside these ranges and needn't reach their ends.
Inputs may be any that keep to these rules, and one draw needn't show every extreme that they name: `index_first`: in each aligned block of 128 samples and in each column, at most 16 indices fall into the range of one block of 1024 factor rows; in every block some range takes exactly 16. `index_second`: in each aligned block of 128 samples and in each column, at most 16 indices fall into the range of one block of 1024 factor rows; in every block some range takes exactly 16.
All inputs are finite; a program needn't handle non-finite values.
Results may differ from the reference program's by a relative error of at most 0.00017.
Values sent between devices are 32-bit elements; how exact they have to be, the bound alone decides.
No kernel may reach another device: no remote copies, remote signals or barrier semaphores. Data moves between devices by JAX's collectives and lax.ppermute only.
A program may use at most 128 MiB of HBM per device.

```python
import jax
import jax.numpy as jnp
from jax import lax

DIM = 16384
RANK = 256
S_DEV = 2048
SAMPLES = 16384
CAP = 16
N_ROW = 16


def owner_block(key, block, most, peers):
    key_first, key_pool, key_order = jax.random.split(key, 3)
    first = jax.random.randint(key_first, (), 0, peers, dtype=jnp.int32)
    others = jnp.arange((peers - 1) * most, dtype=jnp.int32) // most
    others = (first + 1 + others) % peers
    chosen = jax.random.permutation(key_pool, others)[:block - most]
    owners = jnp.concatenate([jnp.full((most,), first, jnp.int32), chosen])
    return jax.random.permutation(key_order, owners)


def draw_pairs(key):
    height = DIM // N_ROW
    block = S_DEV // N_ROW
    blocks = SAMPLES // block
    keys = jax.random.split(key, blocks * 2)
    owners = jax.vmap(lambda one: owner_block(one, block, CAP, N_ROW))(keys)
    owners = owners.reshape(blocks, 2, block).transpose(0, 2, 1).reshape(SAMPLES, 2)
    offsets = jax.random.randint(jax.random.fold_in(key, 99), (SAMPLES, 2), 0, height, dtype=jnp.int32)
    return owners * height + offsets


def draw_index_first(key, part):
    key = jax.random.fold_in(key, 11)
    return draw_pairs(key)


def draw_index_second(key, part):
    key = jax.random.fold_in(key, 23)
    return draw_pairs(key)


def steps_of(own_key, dims, pieces, least, high):
    level, own = 1.0, jax.random.fold_in(own_key, 6)
    for position, blocks in pieces:
        heights = jnp.exp(jax.random.uniform(jax.random.fold_in(own, position), (blocks,), jnp.float32, least / len(pieces), high / len(pieces)))
        level = level * jnp.repeat(heights, dims[position] // blocks).reshape([-1 if axis == position else 1 for axis in range(len(dims))])
    return level


def centred(stream_key, dims, spread, reach, shards=(), held_as=jnp.bfloat16):
    result = spread * jax.random.normal(stream_key, dims, jnp.float32)
    if shards:
        result = result * steps_of(stream_key, dims, shards, -0.22, 0.18)
    return jnp.clip(result, -reach, reach).astype(held_as)


def setup_inputs(seed: int = 0) -> dict:
    key_of = jax.random.split(jax.random.key(seed), 7)
    return {
        "fibres_first": centred(key_of[0], (DIM, SAMPLES), (SAMPLES ** 0.5), 768.0, ((0, 16), (1, 8)), jnp.float32),
        "fibres_second": centred(key_of[1], (DIM, SAMPLES), (SAMPLES ** 0.5), 768.0, ((0, 16), (1, 8)), jnp.float32),
        "index_first": draw_index_first(jax.random.fold_in(key_of[6], 71), 0),
        "index_second": draw_index_second(jax.random.fold_in(key_of[6], 71), 0),
        "factor_b": centred(key_of[4], (DIM, RANK), 1.0, 6.0, ((0, 16),), jnp.float32),
        "factor_c": centred(key_of[5], (DIM, RANK), 1.0, 6.0, ((0, 16),), jnp.float32),
    }


def solve_mode(fibres, khatri):
    gram_matrix = jnp.dot(khatri.T, khatri, precision=lax.Precision.HIGHEST)
    product = jnp.dot(fibres, khatri, precision=lax.Precision.HIGHEST)
    lower_factor = jnp.linalg.cholesky(gram_matrix)
    solved = jax.scipy.linalg.cho_solve((lower_factor, True), product.T).T
    scales = jnp.sqrt(lax.optimization_barrier(jnp.mean(solved * solved, axis=0)) + 1e-06)
    return (solved / scales, scales)

def reference(fibres_first, fibres_second, index_first, index_second, factor_b, factor_c):
    khatri_first = factor_b[index_first[:, 0]] * factor_c[index_first[:, 1]]
    factor_a, scale_first = solve_mode(fibres_first, khatri_first)
    khatri_second = factor_a[index_second[:, 0]] * factor_c[index_second[:, 1]]
    factor_b_new, weights = solve_mode(fibres_second, khatri_second)
    return (factor_a, factor_b_new, weights)
```

```python
import jax
import jax.numpy as jnp
from jax import lax
from jax.experimental import pallas as pl
from jax.experimental.pallas import tpu as pltpu
from jax.sharding import PartitionSpec as P

F32, BF16 = jnp.float32, jnp.bfloat16
CAP = 16
BLOCK = 128
HIGHEST = lax.Precision.HIGHEST
VMEM = pl.BlockSpec(memory_space=pltpu.VMEM)
CORE = [(i, i ^ 1) for i in range(8)]
ALONG_Z = [[c + 2 * z for z in range(4)] for c in range(2)]


def call(kernel, out, *args, flops=0, size=0, **kwargs):
    return pl.pallas_call(
        kernel,
        out_shape=out,
        in_specs=[VMEM] * len(args),
        out_specs=jax.tree.map(lambda _: VMEM, out),
        cost_estimate=pl.CostEstimate(flops=flops, bytes_accessed=size, transcendentals=0),
        compiler_params=pltpu.CompilerParams(vmem_limit_bytes=40 * 2**20),
        **kwargs,
    )(*args)


def shape(*dims, dtype=F32):
    return jax.ShapeDtypeStruct(dims, dtype)


def dot(a, b, dims=(1, 0)):
    return lax.dot_general(a, b, (((dims[0],), (dims[1],)), ((), ())), precision=HIGHEST, preferred_element_type=F32)


def bf16_dot(a, b):
    return jnp.dot(a, b, preferred_element_type=F32)


def halves(x):
    high = x.astype(BF16)
    return high, (x - high.astype(F32)).astype(BF16)


def pick(onehot, x):
    high, rest = x.astype(BF16), x
    total = bf16_dot(onehot, high)
    for _ in range(2):
        rest = rest - high.astype(F32)
        high = rest.astype(BF16)
        total = total + bf16_dot(onehot, high)
    return total


def slots_of(local, height):
    inside = (local >= 0) & (local < height)
    blocks = local.shape[0]
    before = lax.broadcasted_iota(jnp.int32, (BLOCK, BLOCK), 0) < lax.broadcasted_iota(jnp.int32, (BLOCK, BLOCK), 1)
    slot = bf16_dot(jnp.where(inside, 1.0, 0.0).astype(BF16), jnp.where(before, 1.0, 0.0).astype(BF16))
    slot = jnp.where(inside, slot.astype(jnp.int32), -1)
    which = lax.broadcasted_iota(jnp.int32, (blocks, CAP, BLOCK), 1)
    wanted = jnp.where(slot[:, None, :] == which, local[:, None, :] + 1, 0)
    row = jnp.sum(wanted.astype(F32), axis=2, keepdims=True).astype(jnp.int32).reshape(blocks * CAP, 1) - 1
    return jnp.where(row == lax.broadcasted_iota(jnp.int32, (blocks * CAP, height), 1), 1.0, 0.0).astype(BF16)


def select_kernel(columns, index_ref, *refs):
    owned, out_ref = refs[:-1], refs[-1]
    for n, (column, rows) in enumerate(zip(columns, owned)):
        height = rows.shape[0]
        onehot = slots_of(index_ref[column] - lax.axis_index("row") * height, height)
        picked = pick(onehot, rows[...])
        out_ref[:, n * CAP : (n + 1) * CAP, :] = picked.reshape(-1, CAP, picked.shape[-1])


def select(index, columns, *owned):
    blocks, rank = index.shape[1], owned[0].shape[1]
    n = len(columns)
    return call(
        lambda *refs: select_kernel(columns, *refs),
        shape(blocks, n * CAP, rank),
        index,
        *owned,
        flops=n * 6 * blocks * CAP * owned[0].shape[0] * rank,
        size=n * 2**21,
    )


def place_of(index, height):
    eye = lax.broadcasted_iota(jnp.int32, (BLOCK, BLOCK), 0) == lax.broadcasted_iota(jnp.int32, (BLOCK, BLOCK), 1)
    before = lax.broadcasted_iota(jnp.int32, (BLOCK, BLOCK), 1) < lax.broadcasted_iota(jnp.int32, (BLOCK, BLOCK), 0)
    owner = lax.shift_right_logical(index, height.bit_length() - 1)
    owner = jnp.broadcast_to(owner.astype(F32), (BLOCK, BLOCK))
    column = jnp.sum(jnp.where(eye, owner, 0.0), axis=1, keepdims=True)
    slot = jnp.sum(jnp.where((owner == column) & before, 1.0, 0.0), axis=1, keepdims=True)
    return column.astype(jnp.int32), slot.astype(jnp.int32)


def placed_rows(index, got, which, height):
    owners, slots, rank = got.shape
    owner, slot = place_of(index, height)
    target = owner * slots + which * CAP + slot
    onehot = target == lax.broadcasted_iota(jnp.int32, (BLOCK, owners * slots), 1)
    return pick(jnp.where(onehot, 1.0, 0.0).astype(BF16), got.reshape(owners * slots, rank))


def spread(out_ref, block):
    for peer in range(out_ref.shape[0]):
        out_ref[peer] = block


def first_khatri_kernel(height, index_ref, got_ref, out_ref):
    me = pl.ds(lax.axis_index("row"), 1)
    got = got_ref[...]
    rows = [placed_rows(index_ref[c, me, :], got, c, height) for c in range(2)]
    spread(out_ref, rows[0] * rows[1])


def second_khatri_kernel(height, index_ref, got_ref, other_ref, inverse_ref, scale_ref, out_ref):
    me = pl.ds(lax.axis_index("row"), 1)
    rows = placed_rows(index_ref[0, me, :], got_ref[...], 0, height)
    other = placed_rows(index_ref[1, me, :], other_ref[...], 0, height)
    rows = dot(rows, inverse_ref[...]) / scale_ref[...]
    spread(out_ref, rows * other)


def gram_kernel(khatri_ref, out_ref, gram):
    high, low = halves(khatri_ref[...])
    t = lambda a, b: lax.dot_general(a, b, (((0,), (0,)), ((), ())), preferred_element_type=F32)
    cross = t(high, low)
    gram[...] = t(high, high) + (cross + cross.T)
    mine = out_ref.shape[1]
    block = gram[pl.ds(pl.multiple_of(lax.axis_index("row") * mine, mine), mine), :]
    spread(out_ref, block)


def invert_block(tiles):
    n = len(tiles)
    sub = lax.broadcasted_iota(jnp.int32, (8, 128), 0)
    lane = lax.broadcasted_iota(jnp.int32, (8, 128), 1)
    wide = lambda part: jnp.broadcast_to(part, (8, 128))
    for j in range(n):
        t = tiles[j]
        cols = [wide(t[:, 8 * j + k : 8 * j + k + 1]) for k in range(8)]
        in_panel = (lane >= 8 * j) & (lane < 8 * j + 8)
        rows = jnp.where(in_panel, jnp.where(lane == sub + 8 * j, 1.0, 0.0), t)
        for k in range(8):
            inverse = 1.0 / wide(cols[k][k : k + 1, :])
            here = sub == k
            factor = jnp.where(here, 0.0, cols[k])
            row = wide(rows[k : k + 1, :]) * inverse
            rows = jnp.where(here, row, rows - factor * row)
            for m in range(k + 1, 8):
                entry = wide(cols[m][k : k + 1, :]) * inverse
                cols[m] = jnp.where(here, entry, cols[m] - factor * entry)
        spread_rows = [wide(rows[k : k + 1, :]) for k in range(8)]
        for i in range(n):
            if i != j:
                t = tiles[i]
                kept = jnp.where(in_panel, 0.0, t)
                for k in range(8):
                    kept = kept - wide(t[:, 8 * j + k : 8 * j + k + 1]) * spread_rows[k]
                tiles[i] = kept
        tiles[j] = rows
    return jnp.concatenate(tiles, axis=0)


def inverse_kernel(gram_ref, out_ref):
    h = gram_ref.shape[0] // 2
    a = invert_block([gram_ref[8 * i : 8 * i + 8, :h] for i in range(h // 8)])
    w = dot(a, gram_ref[:h, h:])
    out_ref[h:, h:] = gram_ref[h:, h:] - dot(gram_ref[h:, :h], w)
    s = invert_block([out_ref[h + 8 * i : h + 8 * i + 8, h:] for i in range(h // 8)])
    ws = dot(w, s)
    out_ref[h:, h:] = s
    out_ref[:h, h:] = -ws
    out_ref[h:, :h] = -ws.T
    out_ref[:h, :h] = a + dot(ws, w, (1, 1))


def gram_inverse(khatri):
    rank = khatri.shape[1]
    mine = rank // 16
    slices = call(
        gram_kernel,
        shape(8, mine, rank),
        khatri,
        scratch_shapes=[pltpu.VMEM((rank, rank), F32)],
        flops=6 * khatri.size * rank,
        size=4 * khatri.size,
    )
    parts = lax.all_to_all(slices, "samp", 0, 0, tiled=True)
    summed = jnp.broadcast_to(jnp.sum(parts, axis=0)[None], (16, mine, rank))
    gram = lax.all_to_all(summed, "row", 0, 0, tiled=True).reshape(rank, rank)
    return call(inverse_kernel, shape(rank, rank), gram, flops=2 * 10**10, size=2**19)


def product_kernel(fibres_ref, khatri_ref, out_ref, high_ref, low_ref):
    @pl.when(pl.program_id(0) == 0)
    def _():
        high_ref[...], low_ref[...] = halves(khatri_ref[...])

    high, low = halves(fibres_ref[...])
    out_ref[...] = bf16_dot(high, high_ref[...]) + (bf16_dot(high, low_ref[...]) + bf16_dot(low, high_ref[...]))


def product(fibres, khatri, half):
    rows, depth = fibres.shape
    rank = khatri.shape[1]
    steps = rows // 2 // BLOCK
    grid = pltpu.PrefetchScalarGridSpec(
        num_scalar_prefetch=1,
        grid=(steps,),
        in_specs=[
            pl.BlockSpec((BLOCK, depth), lambda i, h: (h[0] * steps + i, 0)),
            pl.BlockSpec((depth, rank), lambda i, h: (0, 0)),
        ],
        out_specs=pl.BlockSpec((BLOCK, rank), lambda i, h: (i, 0)),
        scratch_shapes=[pltpu.VMEM((depth, rank), BF16)] * 2,
    )
    return pl.pallas_call(
        lambda half_ref, *refs: product_kernel(*refs),
        grid_spec=grid,
        out_shape=shape(rows // 2, rank),
        cost_estimate=pl.CostEstimate(flops=6 * rows // 2 * depth * rank, bytes_accessed=2 * rows * depth, transcendentals=0),
        compiler_params=pltpu.CompilerParams(vmem_limit_bytes=40 * 2**20),
    )(half.reshape(1), fibres, khatri)


def summed_product(fibres, khatri):
    core = lax.axis_index("samp") % 2
    given = lax.ppermute(product(fibres, khatri, 1 - core), "samp", CORE)
    kept = product(fibres, khatri, core) + given
    quarters = lax.all_to_all(kept.reshape(4, -1, kept.shape[1]), "samp", 0, 0, axis_index_groups=ALONG_Z, tiled=True)
    mine = jnp.sum(quarters, axis=0)
    own = lax.all_to_all(
        jnp.broadcast_to(mine[None], quarters.shape), "samp", 0, 0, axis_index_groups=ALONG_Z, tiled=True
    ).reshape(kept.shape)
    other = lax.ppermute(own, "samp", CORE)
    return jnp.concatenate([jnp.where(core == 0, own, other), jnp.where(core == 0, other, own)])


def solve_kernel(product_ref, inverse_ref, solved_ref, squares_ref):
    solved = dot(product_ref[...], inverse_ref[...])
    solved_ref[...] = solved
    squares_ref[...] = jnp.broadcast_to(jnp.sum(solved * solved, axis=0, keepdims=True), squares_ref.shape)


def solve(total, inverse):
    rows, rank = total.shape
    solved, squares = call(
        solve_kernel,
        (shape(rows, rank), shape(16, rank)),
        total,
        inverse,
        flops=12 * rows * rank * rank,
        size=8 * rows * rank,
    )
    squares = lax.all_to_all(squares, "row", 0, 0, tiled=True)
    return solved, jnp.sqrt(jnp.sum(squares, axis=0, keepdims=True) / (16 * rows) + 1e-6)


def exchange(rows):
    return lax.all_to_all(rows, "row", 0, 0, tiled=True)


def shards(fibres_first, fibres_second, index_first, index_second, factor_b, factor_c):
    height, rank = factor_b.shape
    by_block = lambda index: index.T.reshape(2, 16, BLOCK)
    first, second = by_block(index_first), by_block(index_second)

    got = exchange(select(first, (0, 1), factor_b, factor_c))
    blocks = call(lambda *refs: first_khatri_kernel(height, *refs), shape(16, BLOCK, rank), first, got, flops=10**8, size=2**22)
    khatri = exchange(blocks).reshape(-1, rank)
    inverse = gram_inverse(khatri)
    total = summed_product(fibres_first, khatri)
    solved, scale = solve(total, inverse)
    factor_a = solved / scale

    other = exchange(select(second, (1,), factor_c))
    got = exchange(select(second, (0,), total))
    blocks = call(
        lambda *refs: second_khatri_kernel(height, *refs),
        shape(16, BLOCK, rank),
        second,
        got,
        other,
        inverse,
        scale,
        flops=10**8,
        size=2**22,
    )
    khatri = exchange(blocks).reshape(-1, rank)
    inverse = gram_inverse(khatri)
    total = summed_product(fibres_second, khatri)
    solved, weights = solve(total, inverse)
    return (factor_a, solved / weights, weights.reshape(rank))


def solution(mesh):
    placed = (P("row", "samp"), P("row", "samp"), P("samp", None), P("samp", None), P("row", None), P("row", None))
    return jax.shard_map(
        shards,
        mesh=mesh,
        in_specs=placed,
        out_specs=(P("row", None), P("row", None), P()),
        check_vma=False,
    )
```

```python
import jax
import jax.numpy as jnp
from jax import lax
from jax.experimental import pallas as pl
from jax.experimental.pallas import tpu as pltpu
from jax.sharding import PartitionSpec as P

F32, BF16 = jnp.float32, jnp.bfloat16
CAP = 16
BLOCK = 128
HIGHEST = lax.Precision.HIGHEST
VMEM = pl.BlockSpec(memory_space=pltpu.VMEM)
CORE = [(i, i ^ 1) for i in range(8)]


def in_plane(down, right):
    return [(row, (row // 4 + down) % 4 * 4 + (row + right) % 4) for row in range(16)]


def along_z(step):
    return [(2 * z + c, (2 * z + 2 * step) % 8 + c) for z in range(4) for c in range(2)]


def call(kernel, out, *args, flops=0, size=0, specs=None, **kwargs):
    return pl.pallas_call(
        kernel,
        out_shape=out,
        in_specs=specs or [VMEM] * len(args),
        out_specs=jax.tree.map(lambda _: VMEM, out),
        cost_estimate=pl.CostEstimate(flops=flops, bytes_accessed=size, transcendentals=0),
        compiler_params=pltpu.CompilerParams(vmem_limit_bytes=32 * 2**20),
        **kwargs,
    )(*args)


def shape(*dims, dtype=F32):
    return jax.ShapeDtypeStruct(dims, dtype)


def dot(a, b, dims=(1, 0)):
    return lax.dot_general(a, b, (((dims[0],), (dims[1],)), ((), ())), precision=HIGHEST, preferred_element_type=F32)


def bf16_dot(a, b):
    return jnp.dot(a, b, preferred_element_type=F32)


def halves(x):
    high = x.astype(BF16)
    return high, (x - high.astype(F32)).astype(BF16)


def pick(onehot, x):
    high, rest = x.astype(BF16), x
    total = bf16_dot(onehot, high)
    for _ in range(2):
        rest = rest - high.astype(F32)
        high = rest.astype(BF16)
        total = total + bf16_dot(onehot, high)
    return total


def position():
    samp = lax.axis_index("samp")
    return lax.shift_right_logical(samp, 1), lax.bitwise_and(samp, 1)


def quarter(place, step):
    return lax.bitwise_and(place + step + 4, 3)


def place_in_row():
    row = lax.axis_index("row")
    return lax.bitwise_and(row, 3), lax.shift_right_logical(row, 2)


def slots_of(index_ref, column, height):
    blocks = index_ref.shape[1] // BLOCK
    wanted = [index_ref[column : column + 1, t * BLOCK : (t + 1) * BLOCK] for t in range(blocks)]
    local = jnp.concatenate(wanted, axis=0) - lax.axis_index("row") * height
    inside = (local >= 0) & (local < height)
    before = lax.broadcasted_iota(jnp.int32, (BLOCK, BLOCK), 0) < lax.broadcasted_iota(jnp.int32, (BLOCK, BLOCK), 1)
    slot = bf16_dot(jnp.where(inside, 1.0, 0.0).astype(BF16), jnp.where(before, 1.0, 0.0).astype(BF16))
    slot = jnp.where(inside, slot.astype(jnp.int32), -1)
    which = lax.broadcasted_iota(jnp.int32, (blocks, CAP, BLOCK), 1)
    wanted = jnp.where(slot[:, None, :] == which, local[:, None, :] + 1, 0)
    row = jnp.sum(wanted.astype(F32), axis=2, keepdims=True).astype(jnp.int32).reshape(blocks * CAP, 1) - 1
    return jnp.where(row == lax.broadcasted_iota(jnp.int32, (blocks * CAP, height), 1), 1.0, 0.0).astype(BF16)


def select_into(out_ref, part, index_ref, column, rows):
    picked = pick(slots_of(index_ref, column, rows.shape[0]), rows)
    out_ref[:, part * CAP : (part + 1) * CAP, :] = picked.reshape(-1, CAP, picked.shape[-1])


def first_select_kernel(index_hbm, b_hbm, c_hbm, out_ref, index_ref, b_ref, c_ref, sems):
    pairs = ((index_hbm, index_ref), (b_hbm, b_ref), (c_hbm, c_ref))
    copies = [pltpu.make_async_copy(src, dst, sems.at[n]) for n, (src, dst) in enumerate(pairs)]
    for copy in copies:
        copy.start()
    copies[0].wait()
    for column, rows in enumerate((b_ref, c_ref)):
        copies[column + 1].wait()
        select_into(out_ref, column, index_ref, column, rows[...])


def first_select(index, b, c):
    args = [pltpu.with_memory_space_constraint(x, pltpu.HBM) for x in (index, b, c)]
    return call(
        first_select_kernel,
        shape(index.shape[1] // BLOCK, 2 * CAP, b.shape[1]),
        *args,
        specs=[pl.BlockSpec(memory_space=pltpu.HBM)] * 3,
        scratch_shapes=[pltpu.VMEM(x.shape, x.dtype) for x in (index, b, c)] + [pltpu.SemaphoreType.DMA((3,))],
        flops=10**9,
        size=2**21,
    )


def place_of(index, height):
    eye = lax.broadcasted_iota(jnp.int32, (BLOCK, BLOCK), 0) == lax.broadcasted_iota(jnp.int32, (BLOCK, BLOCK), 1)
    before = lax.broadcasted_iota(jnp.int32, (BLOCK, BLOCK), 1) < lax.broadcasted_iota(jnp.int32, (BLOCK, BLOCK), 0)
    owner = lax.shift_right_logical(index, height.bit_length() - 1)
    owner = jnp.broadcast_to(owner.astype(F32), (BLOCK, BLOCK))
    column = jnp.sum(jnp.where(eye, owner, 0.0), axis=1, keepdims=True)
    slot = jnp.sum(jnp.where((owner == column) & before, 1.0, 0.0), axis=1, keepdims=True)
    return column.astype(jnp.int32), slot.astype(jnp.int32)


def placed_rows(index_ref, column, got, height):
    owners, slots, rank = got.shape
    me = pl.multiple_of(lax.axis_index("row") * BLOCK, BLOCK)
    owner, slot = place_of(index_ref[column : column + 1, pl.ds(me, BLOCK)], height)
    target = owner * slots + column * CAP + slot
    onehot = target == lax.broadcasted_iota(jnp.int32, (BLOCK, owners * slots), 1)
    return pick(jnp.where(onehot, 1.0, 0.0).astype(BF16), got.reshape(owners * slots, rank))


def first_khatri_kernel(height, index_ref, got_ref, out_ref):
    got = got_ref[...]
    rows = [placed_rows(index_ref, column, got, height) for column in range(2)]
    out_ref[...] = rows[0] * rows[1]


def column_scale(got_ref, at, count):
    squares = jnp.sum(got_ref[:, at : at + 8, :], axis=0)
    return jnp.sqrt(squares[0:1, :] / count + 1e-6)


def second_khatri_kernel(height, index_ref, got_ref, out_ref, scale_ref):
    got = got_ref[...]
    scale = column_scale(got_ref, 2 * CAP, height * got_ref.shape[0])
    scale_ref[...] = jnp.broadcast_to(scale, scale_ref.shape)
    rows = placed_rows(index_ref, 0, got, height) / scale
    out_ref[...] = rows * placed_rows(index_ref, 1, got, height)


def invert_block(tiles):
    n = len(tiles)
    sub = lax.broadcasted_iota(jnp.int32, (8, 128), 0)
    lane = lax.broadcasted_iota(jnp.int32, (8, 128), 1)
    wide = lambda part: jnp.broadcast_to(part, (8, 128))
    for j in range(n):
        t = tiles[j]
        cols = [wide(t[:, 8 * j + k : 8 * j + k + 1]) for k in range(8)]
        in_panel = (lane >= 8 * j) & (lane < 8 * j + 8)
        rows = jnp.where(in_panel, jnp.where(lane == sub + 8 * j, 1.0, 0.0), t)
        for k in range(8):
            inverse = 1.0 / wide(cols[k][k : k + 1, :])
            here = sub == k
            factor = jnp.where(here, 0.0, cols[k])
            row = wide(rows[k : k + 1, :]) * inverse
            rows = jnp.where(here, row, rows - factor * row)
            for m in range(k + 1, 8):
                entry = wide(cols[m][k : k + 1, :]) * inverse
                cols[m] = jnp.where(here, entry, cols[m] - factor * entry)
        spread_rows = [wide(rows[k : k + 1, :]) for k in range(8)]
        for i in range(n):
            if i != j:
                t = tiles[i]
                kept = jnp.where(in_panel, 0.0, t)
                for k in range(8):
                    kept = kept - wide(t[:, 8 * j + k : 8 * j + k + 1]) * spread_rows[k]
                tiles[i] = kept
        tiles[j] = rows
    return jnp.concatenate(tiles, axis=0)


def inverse_kernel(*refs):
    pieces, (out_ref, gram_ref) = refs[:4], refs[4:]
    z, _ = position()
    rows = pieces[0].shape[0] - BLOCK
    for step, piece in enumerate(pieces):
        gram_ref[pl.ds(pl.multiple_of(quarter(z, -step) * rows, rows), rows), :] = piece[BLOCK:, :]
    h = gram_ref.shape[0] // 2
    a = invert_block([gram_ref[8 * i : 8 * i + 8, :h] for i in range(h // 8)])
    w = dot(a, gram_ref[:h, h:])
    out_ref[h:, h:] = gram_ref[h:, h:] - dot(gram_ref[h:, :h], w)
    s = invert_block([out_ref[h + 8 * i : h + 8 * i + 8, h:] for i in range(h // 8)])
    ws = dot(w, s)
    out_ref[h:, h:] = s
    out_ref[:h, h:] = -ws
    out_ref[h:, :h] = -ws.T
    out_ref[:h, :h] = a + dot(ws, w, (1, 1))


def join_kernel(a, b, c, d, out_ref):
    _, y = place_in_row()
    for step, piece in enumerate((a, b, c, d)):
        at = pl.multiple_of(quarter(y, -step) * BLOCK, BLOCK)
        out_ref[pl.ds(at, BLOCK), :] = piece[...]


def columns_of(fibres_ref, beside, held, sems):
    x, y = place_in_row()
    _, rows, depth = held.shape
    copies = [[], []]
    for place in range(4):
        at = pl.multiple_of((4 * place + quarter(x - y + 4, place + beside)) * BLOCK, BLOCK)
        for half in range(2):
            source = fibres_ref.at[half * rows : (half + 1) * rows, pl.ds(at, BLOCK)]
            target = held.at[half, :, place * BLOCK : (place + 1) * BLOCK]
            copies[half].append(pltpu.make_async_copy(source, target, sems.at[half, place]))
    for copy in copies[0] + copies[1]:
        copy.start()
    return copies


def three_dots(high, low, khatri_high, khatri_low):
    return bf16_dot(high, khatri_high) + (bf16_dot(high, khatri_low) + bf16_dot(low, khatri_high))


def gram_of(high, low):
    t = lambda a, b: lax.dot_general(a, b, (((0,), (0,)), ((), ())), preferred_element_type=F32)
    cross = t(high, low)
    return t(high, high) + (cross + cross.T)


def piece_kernel(beside, ahead, fibres_ref, khatri_ref, *refs):
    held, sems = refs[-2:]
    refs = refs[:-2]
    total_in = refs[:2] if beside else ()
    total_ref, gram_ref, *split_refs = refs[len(total_in) :]
    copies = columns_of(fibres_ref, beside, held.at[0], sems.at[0])
    later = columns_of(fibres_ref, ahead, held.at[1], sems.at[1]) if ahead else ()
    khatri = halves(khatri_ref[...])
    gram = gram_of(*khatri)
    gram_ref[...] = gram + total_in[1][...] if beside else gram
    _, rows, depth = held.at[0].shape
    for half in range(2):
        for copy in copies[half]:
            copy.wait()
        part = three_dots(*halves(held[0, half]), *khatri)
        mine = slice(half * rows, (half + 1) * rows)
        total_ref[mine, :] = part + total_in[0][mine, :] if beside else part
    for half in range(2 if ahead else 0):
        for copy in later[half]:
            copy.wait()
        mine = slice(half * rows, (half + 1) * rows)
        split_refs[0][mine, :], split_refs[1][mine, :] = halves(held[1, half])


def half_of(high_ref, low_ref, khatri, total_ref, core, out_ref):
    rows = high_ref.shape[0] // 2
    mine = pl.ds(pl.multiple_of(core * rows, rows), rows)
    total = three_dots(high_ref[mine, :], low_ref[mine, :], *khatri) + total_ref[mine, :]
    for place in range(4):
        out_ref[place, :BLOCK, :] = total[place * BLOCK : (place + 1) * BLOCK]


def given_kernel(high_ref, low_ref, khatri_ref, total_ref, gram_ref, out_ref):
    _, core = position()
    khatri = halves(khatri_ref[...])
    half_of(high_ref, low_ref, khatri, total_ref, 1 - core, out_ref)
    gram = gram_of(*khatri) + gram_ref[...]
    rows = gram.shape[0] // 4
    for place in range(4):
        out_ref[place, BLOCK:, :] = gram[place * rows : (place + 1) * rows]


def kept_kernel(high_ref, low_ref, khatri_ref, total_ref, given_ref, out_ref):
    _, core = position()
    half_of(high_ref, low_ref, halves(khatri_ref[...]), total_ref, core, out_ref)
    out_ref[:, BLOCK:, :] = given_ref[:, BLOCK:, :]


def pair_kernel(kept_ref, given_ref, *outs):
    z, _ = position()
    for step, out_ref in enumerate(outs):
        place = quarter(z, step)
        out_ref[...] = kept_ref[place] + given_ref[place]


def quarter_kernel(a, b, c, d, out_ref):
    out_ref[...] = (a[...] + b[...]) + (c[...] + d[...])


def sums_over_row_group(fibres, block):
    rank = block.shape[1]
    rows, samples = fibres.shape
    depth = samples // 4
    flops = 6 * rows * depth * rank
    fibres = pltpu.with_memory_space_constraint(fibres, pltpu.HBM)
    blocks = [block] + [lax.ppermute(block, "row", in_plane(step, step)) for step in (1, 2, 3)]
    piece = call(join_kernel, shape(depth, rank), *blocks, size=2**20)
    moves = {-1: (0, 1), 1: (0, -1), 2: (2, 0)}
    pieces = {beside: lax.ppermute(piece, "row", in_plane(*move)) for beside, move in moves.items()}
    pieces[0] = piece
    state = ()
    for beside, ahead in ((0, 0), (-1, 0), (1, 2)):
        out = (shape(rows, rank), shape(rank, rank))
        split = (shape(rows, depth, dtype=BF16),) * 2 if ahead else ()
        state = call(
            lambda *refs, beside=beside, ahead=ahead: piece_kernel(beside, ahead, *refs),
            out + split,
            fibres,
            pieces[beside],
            *state,
            specs=[pl.BlockSpec(memory_space=pltpu.HBM)] + [VMEM] * (1 + len(state)),
            scratch_shapes=[pltpu.VMEM((2, 2, rows // 2, depth), F32), pltpu.SemaphoreType.DMA((2, 2, 4))],
            flops=flops,
            size=2**22,
        )
    total, gram, high, low = state
    out = shape(4, BLOCK + rank // 4, rank)
    given = call(given_kernel, out, high, low, pieces[2], total, gram, flops=flops, size=2**21)
    got = lax.ppermute(given, "samp", CORE)
    kept = call(kept_kernel, out, high, low, pieces[2], total, given, flops=flops // 2, size=2**21)
    return kept, got


def summed(fibres, block):
    rank = block.shape[1]
    kept, got = sums_over_row_group(fibres, block)
    rows = kept.shape[1]
    pairs = call(pair_kernel, (shape(rows, rank),) * 4, kept, got, size=2**21)
    parts = [pairs[0]] + [lax.ppermute(pairs[step], "samp", along_z(step)) for step in (1, 2, 3)]
    mine = call(quarter_kernel, shape(rows, rank), *parts, size=2**20)
    pieces = [mine] + [lax.ppermute(mine, "samp", along_z(step)) for step in (1, 2, 3)]
    others = [lax.ppermute(piece, "samp", CORE) for piece in pieces]
    inverse = call(
        inverse_kernel,
        shape(rank, rank),
        *pieces,
        scratch_shapes=[pltpu.VMEM((rank, rank), F32)],
        flops=10**10,
        size=2**19,
    )
    return pieces + others, inverse


def solve_pieces(pieces, inverse_ref, product, solved_ref):
    z, core = position()
    for n, piece in enumerate(pieces):
        owner = core if n < 4 else 1 - core
        at = owner * (4 * BLOCK) + quarter(z, -(n % 4)) * BLOCK
        product[pl.ds(pl.multiple_of(at, BLOCK), BLOCK), :] = piece[:BLOCK, :]
    solved_ref[...] = dot(product[...], inverse_ref[...])
    solved = solved_ref[...]
    return jnp.sum(solved * solved, axis=0, keepdims=True)


def first_solve_kernel(*refs):
    pieces, (inverse_ref, index_ref, c_ref, solved_ref, out_ref, product) = refs[:8], refs[8:]
    squares = solve_pieces(pieces, inverse_ref, product, solved_ref)
    peers, _, rank = out_ref.shape
    out_ref[:, 2 * CAP :, :] = jnp.broadcast_to(squares[None], (peers, 8, rank))
    select_into(out_ref, 0, index_ref, 0, solved_ref[...])
    select_into(out_ref, 1, index_ref, 1, c_ref[...])


def second_solve_kernel(*refs):
    pieces, (inverse_ref, solved_ref, out_ref, product) = refs[:8], refs[8:]
    squares = solve_pieces(pieces, inverse_ref, product, solved_ref)
    out_ref[...] = jnp.broadcast_to(squares[None], out_ref.shape)


def finish_kernel(solved_ref, got_ref, out_ref, scale_ref):
    scale = column_scale(got_ref, 0, solved_ref.shape[0] * got_ref.shape[0])
    scale_ref[...] = jnp.broadcast_to(scale, scale_ref.shape)
    out_ref[...] = solved_ref[...] / scale


def exchange(rows):
    return lax.all_to_all(rows, "row", 0, 0, tiled=True)


def shards(fibres_first, fibres_second, index_first, index_second, factor_b, factor_c):
    height, rank = factor_b.shape
    peers = index_first.shape[0] // BLOCK
    first, second = index_first.T, index_second.T
    scratch = [pltpu.VMEM((height, rank), F32)]

    got = exchange(first_select(first, factor_b, factor_c))
    block = call(lambda *refs: first_khatri_kernel(height, *refs), shape(BLOCK, rank), first, got, flops=10**8, size=2**22)
    pieces, inverse = summed(fibres_first, block)
    solved, sent = call(
        first_solve_kernel,
        (shape(height, rank), shape(peers, 2 * CAP + 8, rank)),
        *pieces,
        inverse,
        second,
        factor_c,
        scratch_shapes=scratch,
        flops=10**9,
        size=2**21,
    )
    block, scale = call(
        lambda *refs: second_khatri_kernel(height, *refs),
        (shape(BLOCK, rank), shape(8, rank)),
        second,
        exchange(sent),
        flops=10**8,
        size=2**22,
    )
    pieces, inverse = summed(fibres_second, block)
    solved, _ = lax.optimization_barrier((solved, pieces[0]))
    factor_a = solved / scale[:1]
    solved, sent = call(
        second_solve_kernel,
        (shape(height, rank), shape(peers, 8, rank)),
        *pieces,
        inverse,
        scratch_shapes=scratch,
        flops=10**9,
        size=2**21,
    )
    sent, factor_a = lax.optimization_barrier((sent, factor_a))
    factor_b_new, weights = call(finish_kernel, (shape(height, rank), shape(8, rank)), solved, exchange(sent), size=2**21)
    return (factor_a, factor_b_new, weights[0])


def solution(mesh):
    placed = (P("row", "samp"), P("row", "samp"), P("samp", None), P("samp", None), P("row", None), P("row", None))
    return jax.shard_map(
        shards,
        mesh=mesh,
        in_specs=placed,
        out_specs=(P("row", None), P("row", None), P()),
        check_vma=False,
    )
```

```python
import jax
import jax.numpy as jnp
from jax import lax
from jax.experimental import pallas as pl
from jax.experimental.pallas import tpu as pltpu
from jax.sharding import PartitionSpec as P

F32, BF16 = jnp.float32, jnp.bfloat16
CAP = 16
BLOCK = 128
HIGHEST = lax.Precision.HIGHEST
VMEM = pl.BlockSpec(memory_space=pltpu.VMEM)
CORE = [(i, i ^ 1) for i in range(8)]
FAR_FIRST = (2, 1, 3)


def in_plane(down, right):
    return [(row, (row // 4 + down) % 4 * 4 + (row + right) % 4) for row in range(16)]


def along_z(step):
    return [(2 * z + c, (2 * z + 2 * step) % 8 + c) for z in range(4) for c in range(2)]


def call(kernel, out, *args, flops=0, size=0, specs=None, **kwargs):
    return pl.pallas_call(
        kernel,
        out_shape=out,
        in_specs=specs or [VMEM] * len(args),
        out_specs=jax.tree.map(lambda _: VMEM, out),
        cost_estimate=pl.CostEstimate(flops=flops, bytes_accessed=size, transcendentals=0),
        compiler_params=pltpu.CompilerParams(vmem_limit_bytes=32 * 2**20),
        **kwargs,
    )(*args)


def shape(*dims, dtype=F32):
    return jax.ShapeDtypeStruct(dims, dtype)


def dot(a, b, dims=(1, 0)):
    return lax.dot_general(a, b, (((dims[0],), (dims[1],)), ((), ())), precision=HIGHEST, preferred_element_type=F32)


def bf16_dot(a, b):
    return jnp.dot(a, b, preferred_element_type=F32)


def halves(x):
    high = x.astype(BF16)
    return high, (x - high.astype(F32)).astype(BF16)


def pick(onehot, x):
    high, low = halves(x)
    return bf16_dot(onehot, high) + bf16_dot(onehot, low)


def position():
    samp = lax.axis_index("samp")
    return lax.shift_right_logical(samp, 1), lax.bitwise_and(samp, 1)


def quarter(place, step):
    return lax.bitwise_and(place + step + 4, 3)


def place_in_row():
    row = lax.axis_index("row")
    return lax.bitwise_and(row, 3), lax.shift_right_logical(row, 2)


def slots_of(index_ref, column, height):
    blocks = index_ref.shape[1] // BLOCK
    wanted = [index_ref[column : column + 1, t * BLOCK : (t + 1) * BLOCK] for t in range(blocks)]
    local = jnp.concatenate(wanted, axis=0) - lax.axis_index("row") * height
    inside = (local >= 0) & (local < height)
    before = lax.broadcasted_iota(jnp.int32, (BLOCK, BLOCK), 0) < lax.broadcasted_iota(jnp.int32, (BLOCK, BLOCK), 1)
    slot = bf16_dot(jnp.where(inside, 1.0, 0.0).astype(BF16), jnp.where(before, 1.0, 0.0).astype(BF16))
    slot = jnp.where(inside, slot.astype(jnp.int32), -1)
    which = lax.broadcasted_iota(jnp.int32, (blocks, CAP, BLOCK), 1)
    wanted = jnp.where(slot[:, None, :] == which, local[:, None, :] + 1, 0)
    row = jnp.sum(wanted.astype(F32), axis=2, keepdims=True).astype(jnp.int32).reshape(blocks * CAP, 1) - 1
    return jnp.where(row == lax.broadcasted_iota(jnp.int32, (blocks * CAP, height), 1), 1.0, 0.0).astype(BF16)


def select_into(out_ref, part, onehot, rows):
    picked = pick(onehot, rows)
    out_ref[:, part * CAP : (part + 1) * CAP, :] = picked.reshape(-1, CAP, picked.shape[-1])


def first_select_kernel(index_hbm, b_hbm, c_hbm, out_ref, index_out, index_ref, b_ref, c_ref, sems):
    pairs = ((index_hbm, index_ref), (b_hbm, b_ref), (c_hbm, c_ref))
    copies = [pltpu.make_async_copy(src, dst, sems.at[n]) for n, (src, dst) in enumerate(pairs)]
    for copy in copies:
        copy.start()
    copies[0].wait()
    index_out[...] = index_ref[...]
    onehots = [slots_of(index_ref, column, b_ref.shape[0]) for column in range(2)]
    for column, rows in enumerate((b_ref, c_ref)):
        copies[column + 1].wait()
        select_into(out_ref, column, onehots[column], rows[...])


def first_select(index, b, c):
    args = [pltpu.with_memory_space_constraint(x, pltpu.HBM) for x in (index, b, c)]
    return call(
        first_select_kernel,
        (shape(index.shape[1] // BLOCK, 2 * CAP, b.shape[1]), shape(*index.shape, dtype=jnp.int32)),
        *args,
        specs=[pl.BlockSpec(memory_space=pltpu.HBM)] * 3,
        scratch_shapes=[pltpu.VMEM(x.shape, x.dtype) for x in (index, b, c)] + [pltpu.SemaphoreType.DMA((3,))],
        flops=10**9,
        size=2**21,
    )


def place_of(index, height):
    eye = lax.broadcasted_iota(jnp.int32, (BLOCK, BLOCK), 0) == lax.broadcasted_iota(jnp.int32, (BLOCK, BLOCK), 1)
    before = lax.broadcasted_iota(jnp.int32, (BLOCK, BLOCK), 1) < lax.broadcasted_iota(jnp.int32, (BLOCK, BLOCK), 0)
    owner = lax.shift_right_logical(index, height.bit_length() - 1)
    owner = jnp.broadcast_to(owner.astype(F32), (BLOCK, BLOCK))
    column = jnp.sum(jnp.where(eye, owner, 0.0), axis=1, keepdims=True)
    slot = jnp.sum(jnp.where((owner == column) & before, 1.0, 0.0), axis=1, keepdims=True)
    return column.astype(jnp.int32), slot.astype(jnp.int32)


def placed_rows(index_ref, column, got, height):
    owners, slots, rank = got.shape
    me = pl.multiple_of(lax.axis_index("row") * BLOCK, BLOCK)
    owner, slot = place_of(index_ref[column : column + 1, pl.ds(me, BLOCK)], height)
    target = owner * slots + column * CAP + slot
    onehot = target == lax.broadcasted_iota(jnp.int32, (BLOCK, owners * slots), 1)
    return pick(jnp.where(onehot, 1.0, 0.0).astype(BF16), got.reshape(owners * slots, rank))


def first_khatri_kernel(height, index_ref, got_ref, out_ref):
    got = got_ref[...]
    rows = [placed_rows(index_ref, column, got, height) for column in range(2)]
    out_ref[...] = rows[0] * rows[1]


def column_scale(got_ref, at, count):
    squares = jnp.sum(got_ref[:, at : at + 8, :], axis=0)
    return jnp.sqrt(squares[0:1, :] / count + 1e-6)


def second_khatri_kernel(height, index_ref, got_ref, out_ref, scale_ref):
    got = got_ref[...]
    scale = column_scale(got_ref, 2 * CAP, height * got_ref.shape[0])
    scale_ref[...] = jnp.broadcast_to(scale, scale_ref.shape)
    rows = placed_rows(index_ref, 0, got, height) / scale
    out_ref[...] = rows * placed_rows(index_ref, 1, got, height)


GROUP = 4


def invert_block(tiles):
    sub = lax.broadcasted_iota(jnp.int32, (8, 128), 0)
    lane = lax.broadcasted_iota(jnp.int32, (8, 128), 1)
    wide = lambda part: jnp.broadcast_to(part, (8, 128))

    def group(_, tiles):
        tiles = list(tiles)
        for j in range(GROUP):
            t = tiles[j]
            cols = [wide(t[:, 8 * j + k : 8 * j + k + 1]) for k in range(8)]
            in_panel = (lane >= 8 * j) & (lane < 8 * j + 8)
            rows = jnp.where(in_panel, jnp.where(lane == sub + 8 * j, 1.0, 0.0), t)
            for k in range(8):
                inverse = 1.0 / wide(cols[k][k : k + 1, :])
                here = sub == k
                factor = jnp.where(here, 0.0, cols[k])
                row = wide(rows[k : k + 1, :]) * inverse
                rows = jnp.where(here, row, rows - factor * row)
                for m in range(k + 1, 8):
                    entry = wide(cols[m][k : k + 1, :]) * inverse
                    cols[m] = jnp.where(here, entry, cols[m] - factor * entry)
            spread_rows = [wide(rows[k : k + 1, :]) for k in range(8)]
            for i in list(range(j + 1, len(tiles))) + list(range(j)):
                t = tiles[i]
                kept = jnp.where(in_panel, 0.0, t)
                for k in range(8):
                    kept = kept - wide(t[:, 8 * j + k : 8 * j + k + 1]) * spread_rows[k]
                tiles[i] = kept
            tiles[j] = rows
        tiles = [pltpu.roll(t, 128 - 8 * GROUP, 1) for t in tiles]
        return tuple(tiles[GROUP:] + tiles[:GROUP])

    return jnp.concatenate(lax.fori_loop(0, len(tiles) // GROUP, group, tuple(tiles)), axis=0)


def first_inverse_kernel(*refs):
    pieces, (a_ref, w_ref, rest_ref, gram_ref) = refs[:4], refs[4:]
    z, _ = position()
    rows = pieces[0].shape[0]
    for step, piece in enumerate(pieces):
        gram_ref[pl.ds(pl.multiple_of(quarter(z, -step) * rows, rows), rows), :] = piece[...]
    h = gram_ref.shape[0] // 2
    a_ref[...] = invert_block([gram_ref[8 * i : 8 * i + 8, :h] for i in range(h // 8)])
    w_ref[...] = dot(a_ref[...], gram_ref[:h, h:])
    rest_ref[...] = gram_ref[h:, h:] - dot(gram_ref[h:, :h], w_ref[...])


def second_inverse_kernel(a_ref, w_ref, rest_ref, out_ref):
    h = a_ref.shape[0]
    s = invert_block([rest_ref[8 * i : 8 * i + 8, :] for i in range(h // 8)])
    ws = dot(w_ref[...], s)
    out_ref[h:, h:] = s
    out_ref[:h, h:] = -ws
    out_ref[h:, :h] = -ws.T
    out_ref[:h, :h] = a_ref[...] + dot(ws, w_ref[...], (1, 1))


def join_kernel(place, a, b, c, d, out_ref):
    for step, piece in enumerate((a, b, c, d)):
        at = pl.multiple_of(quarter(place(), -step) * BLOCK, BLOCK)
        out_ref[pl.ds(at, BLOCK), :] = piece[...]


def joined(pieces, place):
    rows, rank = pieces[0].shape
    return call(lambda *refs: join_kernel(place, *refs), shape(4 * rows, rank), *pieces, size=2**20)


DIAGONALS = (0, -1, 1, 2)


def split_kernel(fibres_ref, *refs):
    outs, (held, sems) = refs[:8], refs[8:]
    x, y = place_in_row()
    _, _, rows, _ = held.shape
    copies = []
    for n, beside in enumerate(DIAGONALS):
        for half in range(2):
            copies.append([])
            for place in range(4):
                at = pl.multiple_of((4 * place + quarter(x - y + 4, place + beside)) * BLOCK, BLOCK)
                source = fibres_ref.at[half * rows : (half + 1) * rows, pl.ds(at, BLOCK)]
                target = held.at[n, half, :, place * BLOCK : (place + 1) * BLOCK]
                copies[-1].append(pltpu.make_async_copy(source, target, sems.at[n, half, place]))
                copies[-1][-1].start()
    for n in range(4):
        for half in range(2):
            for copy in copies[2 * n + half]:
                copy.wait()
            mine = slice(half * rows, (half + 1) * rows)
            outs[2 * n][mine, :], outs[2 * n + 1][mine, :] = halves(held[n, half])


def split(fibres):
    rows, samples = fibres.shape
    depth = samples // 4
    return call(
        split_kernel,
        (shape(rows, depth, dtype=BF16),) * 8,
        pltpu.with_memory_space_constraint(fibres, pltpu.HBM),
        specs=[pl.BlockSpec(memory_space=pltpu.HBM)],
        scratch_shapes=[pltpu.VMEM((4, 2, rows // 2, depth), F32), pltpu.SemaphoreType.DMA((4, 2, 4))],
        flops=4 * fibres.size,
        size=8 * fibres.size,
    )


def three_dots(high, low, khatri_high, khatri_low):
    return bf16_dot(high, khatri_high) + (bf16_dot(high, khatri_low) + bf16_dot(low, khatri_high))


def gram_of(high, low):
    t = lambda a, b: lax.dot_general(a, b, (((0,), (0,)), ((), ())), preferred_element_type=F32)
    cross = t(high, low)
    return t(high, high) + (cross + cross.T)


def piece_kernel(high_ref, low_ref, khatri_ref, *refs):
    so_far, (total_ref, gram_ref) = refs[:-2], refs[-2:]
    khatri = halves(khatri_ref[...])
    total, gram = three_dots(high_ref[...], low_ref[...], *khatri), gram_of(*khatri)
    total_ref[...] = total + so_far[0][...] if so_far else total
    gram_ref[...] = gram + so_far[1][...] if so_far else gram


def half_of(high_ref, low_ref, khatri, total_ref, core, out_ref):
    rows = high_ref.shape[0] // 2
    mine = pl.ds(pl.multiple_of(core * rows, rows), rows)
    total = three_dots(high_ref[mine, :], low_ref[mine, :], *khatri) + total_ref[mine, :]
    for place in range(4):
        out_ref[place, :BLOCK, :] = total[place * BLOCK : (place + 1) * BLOCK]


def given_kernel(high_ref, low_ref, khatri_ref, total_ref, gram_ref, out_ref):
    _, core = position()
    khatri = halves(khatri_ref[...])
    half_of(high_ref, low_ref, khatri, total_ref, 1 - core, out_ref)
    gram = gram_of(*khatri) + gram_ref[...]
    rows = gram.shape[0] // 4
    for place in range(4):
        out_ref[place, BLOCK:, :] = gram[place * rows : (place + 1) * rows]


def kept_kernel(high_ref, low_ref, khatri_ref, total_ref, given_ref, out_ref):
    _, core = position()
    half_of(high_ref, low_ref, halves(khatri_ref[...]), total_ref, core, out_ref)
    out_ref[:, BLOCK:, :] = given_ref[:, BLOCK:, :]


def pair_kernel(kept_ref, given_ref, *outs):
    z, _ = position()
    for step, out_ref in enumerate(outs):
        place = quarter(z, step)
        out_ref[...] = kept_ref[place] + given_ref[place]


def quarter_kernel(a, b, c, d, product_ref, gram_ref):
    total = (a[...] + b[...]) + (c[...] + d[...])
    product_ref[...] = total[:BLOCK]
    gram_ref[...] = total[BLOCK:]


def from_z(own):
    got = {step: lax.ppermute(own, "samp", along_z(step)) for step in FAR_FIRST}
    return [own, got[1], got[2], got[3]]


def sums_over_row_group(fibres, block, aside):
    rank = block.shape[1]
    rows, samples = fibres.shape
    depth = samples // 4
    flops = 6 * rows * depth * rank
    near = {step: lax.ppermute(block, "row", in_plane(step, step)) for step in FAR_FIRST}
    piece = joined([block, near[1], near[2], near[3]], lambda: place_in_row()[1])
    fibres, piece = lax.optimization_barrier((fibres, piece))
    parts = split(fibres)
    moves = {-1: (0, 1), 1: (0, -1), 2: (2, 0)}
    pieces = {beside: lax.ppermute(piece, "row", in_plane(*move)) for beside, move in moves.items()}
    pieces[0] = piece
    state = ()
    for n, beside in enumerate(DIAGONALS[:3]):
        high, low = parts[2 * n : 2 * n + 2]
        out = (shape(rows, rank), shape(rank, rank))
        state = call(piece_kernel, out, high, low, pieces[beside], *state, flops=flops, size=2**22)
        if n == 0:
            state, extra = lax.optimization_barrier((state, aside(piece)))
    total, gram = state
    high, low = parts[6:]
    out = shape(4, BLOCK + rank // 4, rank)
    given = call(given_kernel, out, high, low, pieces[2], total, gram, flops=flops, size=2**21)
    got = lax.ppermute(given, "samp", CORE)
    kept = call(kept_kernel, out, high, low, pieces[2], total, given, flops=flops // 2, size=2**21)
    return kept, got, extra


def summed(fibres, block, aside):
    rank = block.shape[1]
    kept, got, extra = sums_over_row_group(fibres, block, aside)
    rows = kept.shape[1]
    pairs = call(pair_kernel, (shape(rows, rank),) * 4, kept, got, size=2**21)
    parts = [pairs[0]] + [lax.ppermute(pairs[step], "samp", along_z(step)) for step in FAR_FIRST]
    product, gram = call(quarter_kernel, (shape(BLOCK, rank), shape(rank // 4, rank)), *parts, size=2**20)
    h = rank // 2
    first = call(
        first_inverse_kernel,
        (shape(h, h),) * 3,
        *from_z(gram),
        scratch_shapes=[pltpu.VMEM((rank, rank), F32)],
        flops=10**11,
        size=2**19,
    )
    first, pieces = lax.optimization_barrier((first, from_z(product)))
    mine = joined(pieces, lambda: position()[0])
    other = lax.ppermute(mine, "samp", CORE)
    inverse = call(second_inverse_kernel, shape(rank, rank), *first, flops=10**11, size=2**19)
    return mine, other, inverse, extra


def solve_into(out_ref, mine_ref, other_ref, inverse_ref):
    _, core = position()
    inverse = halves(inverse_ref[...])
    rows = mine_ref.shape[0]
    for owner, ref in ((core, mine_ref), (1 - core, other_ref)):
        out_ref[pl.ds(pl.multiple_of(owner * rows, rows), rows), :] = three_dots(*halves(ref[...]), *inverse)


def select_kernel(index_ref, c_ref, out_ref):
    select_into(out_ref, 0, slots_of(index_ref, 1, c_ref.shape[0]), c_ref[...])


def first_solve_kernel(mine_ref, other_ref, inverse_ref, index_ref, chosen_ref, solved_ref, out_ref):
    solve_into(solved_ref, mine_ref, other_ref, inverse_ref)
    solved = solved_ref[...]
    peers, _, rank = out_ref.shape
    squares = jnp.sum(solved * solved, axis=0, keepdims=True)
    out_ref[:, 2 * CAP :, :] = jnp.broadcast_to(squares[None], (peers, 8, rank))
    out_ref[:, CAP : 2 * CAP, :] = chosen_ref[...]
    select_into(out_ref, 0, slots_of(index_ref, 0, solved.shape[0]), solved)


def second_solve_kernel(mine_ref, other_ref, inverse_ref, solved_ref, out_ref):
    solve_into(solved_ref, mine_ref, other_ref, inverse_ref)
    solved = solved_ref[...]
    out_ref[...] = jnp.broadcast_to(jnp.sum(solved * solved, axis=0, keepdims=True)[None], out_ref.shape)


def finish_kernel(solved_ref, got_ref, out_ref, scale_ref):
    scale = column_scale(got_ref, 0, solved_ref.shape[0] * got_ref.shape[0])
    scale_ref[...] = jnp.broadcast_to(scale, scale_ref.shape)
    out_ref[...] = solved_ref[...] / scale


def exchange(rows):
    return lax.all_to_all(rows, "row", 0, 0, tiled=True)


def shards(fibres_first, fibres_second, index_first, index_second, factor_b, factor_c):
    height, rank = factor_b.shape
    peers = index_first.shape[0] // BLOCK
    first, second = index_first.T, index_second.T

    sent, first = first_select(first, factor_b, factor_c)
    got = exchange(sent)
    block = call(lambda *refs: first_khatri_kernel(height, *refs), shape(BLOCK, rank), first, got, flops=10**8, size=2**22)

    def choose(piece):
        index, rows, _ = lax.optimization_barrier((second, factor_c, piece))
        return call(select_kernel, shape(peers, CAP, rank), index, rows, flops=10**9, size=2**21)

    mine, other, inverse, chosen = summed(fibres_first, block, choose)
    solved, sent = call(
        first_solve_kernel,
        (shape(height, rank), shape(peers, 2 * CAP + 8, rank)),
        mine,
        other,
        inverse,
        second,
        chosen,
        flops=10**9,
        size=2**21,
    )
    block, scale = call(
        lambda *refs: second_khatri_kernel(height, *refs),
        (shape(BLOCK, rank), shape(8, rank)),
        second,
        exchange(sent),
        flops=10**8,
        size=2**22,
    )

    def normalise(piece):
        rows, _ = lax.optimization_barrier((solved, piece))
        return rows / scale[:1]

    mine, other, inverse, factor_a = summed(fibres_second, block, normalise)
    solved, sent = call(
        second_solve_kernel,
        (shape(height, rank), shape(peers, 8, rank)),
        mine,
        other,
        inverse,
        flops=10**9,
        size=2**21,
    )
    factor_b_new, weights = call(finish_kernel, (shape(height, rank), shape(8, rank)), solved, exchange(sent), size=2**21)
    return (factor_a, factor_b_new, weights[0])


def solution(mesh):
    placed = (P("row", "samp"), P("row", "samp"), P("samp", None), P("samp", None), P("row", None), P("row", None))
    return jax.shard_map(
        shards,
        mesh=mesh,
        in_specs=placed,
        out_specs=(P("row", None), P("row", None), P()),
        check_vma=False,
    )
```

```python
import jax
import jax.numpy as jnp
from jax import lax
from jax.experimental import pallas as pl
from jax.experimental.pallas import tpu as pltpu
from jax.sharding import PartitionSpec as P

F32, BF16 = jnp.float32, jnp.bfloat16
CAP = 16
BLOCK = 128
HIGHEST = lax.Precision.HIGHEST
VMEM = pl.BlockSpec(memory_space=pltpu.VMEM)
CORE = [(i, i ^ 1) for i in range(8)]
FAR_FIRST = (2, 1, 3)


def in_plane(down, right):
    return [(row, (row // 4 + down) % 4 * 4 + (row + right) % 4) for row in range(16)]


def along_z(step):
    return [(2 * z + c, (2 * z + 2 * step) % 8 + c) for z in range(4) for c in range(2)]


def call(kernel, out, *args, flops=0, size=0, specs=None, **kwargs):
    return pl.pallas_call(
        kernel,
        out_shape=out,
        in_specs=specs or [VMEM] * len(args),
        out_specs=jax.tree.map(lambda _: VMEM, out),
        cost_estimate=pl.CostEstimate(flops=flops, bytes_accessed=size, transcendentals=0),
        compiler_params=pltpu.CompilerParams(vmem_limit_bytes=32 * 2**20),
        **kwargs,
    )(*args)


def shape(*dims, dtype=F32):
    return jax.ShapeDtypeStruct(dims, dtype)


def dot(a, b, dims=(1, 0)):
    return lax.dot_general(a, b, (((dims[0],), (dims[1],)), ((), ())), precision=HIGHEST, preferred_element_type=F32)


def bf16_dot(a, b):
    return jnp.dot(a, b, preferred_element_type=F32)


def halves(x):
    high = x.astype(BF16)
    return high, (x - high.astype(F32)).astype(BF16)


def pick(onehot, x):
    high, low = halves(x)
    return bf16_dot(onehot, high) + bf16_dot(onehot, low)


def position():
    samp = lax.axis_index("samp")
    return lax.shift_right_logical(samp, 1), lax.bitwise_and(samp, 1)


def quarter(place, step):
    return lax.bitwise_and(place + step + 4, 3)


def place_in_row():
    row = lax.axis_index("row")
    return lax.bitwise_and(row, 3), lax.shift_right_logical(row, 2)


def slots_of(index_ref, column, height):
    blocks = index_ref.shape[1] // BLOCK
    wanted = [index_ref[column : column + 1, t * BLOCK : (t + 1) * BLOCK] for t in range(blocks)]
    local = jnp.concatenate(wanted, axis=0) - lax.axis_index("row") * height
    inside = (local >= 0) & (local < height)
    before = lax.broadcasted_iota(jnp.int32, (BLOCK, BLOCK), 0) < lax.broadcasted_iota(jnp.int32, (BLOCK, BLOCK), 1)
    slot = bf16_dot(jnp.where(inside, 1.0, 0.0).astype(BF16), jnp.where(before, 1.0, 0.0).astype(BF16))
    slot = jnp.where(inside, slot.astype(jnp.int32), -1)
    which = lax.broadcasted_iota(jnp.int32, (blocks, CAP, BLOCK), 1)
    wanted = jnp.where(slot[:, None, :] == which, local[:, None, :] + 1, 0)
    row = jnp.sum(wanted.astype(F32), axis=2, keepdims=True).astype(jnp.int32).reshape(blocks * CAP, 1) - 1
    return jnp.where(row == lax.broadcasted_iota(jnp.int32, (blocks * CAP, height), 1), 1.0, 0.0).astype(BF16)


def select_into(out_ref, part, onehot, rows):
    picked = pick(onehot, rows)
    out_ref[:, part * CAP : (part + 1) * CAP, :] = picked.reshape(-1, CAP, picked.shape[-1])


def first_select_kernel(index_hbm, b_hbm, c_hbm, out_ref, index_out, index_ref, b_ref, c_ref, sems):
    pairs = ((index_hbm, index_ref), (b_hbm, b_ref), (c_hbm, c_ref))
    copies = [pltpu.make_async_copy(src, dst, sems.at[n]) for n, (src, dst) in enumerate(pairs)]
    for copy in copies:
        copy.start()
    copies[0].wait()
    index_out[...] = index_ref[...]
    onehots = [slots_of(index_ref, column, b_ref.shape[0]) for column in range(2)]
    for column, rows in enumerate((b_ref, c_ref)):
        copies[column + 1].wait()
        select_into(out_ref, column, onehots[column], rows[...])


def first_select(index, b, c):
    args = [pltpu.with_memory_space_constraint(x, pltpu.HBM) for x in (index, b, c)]
    return call(
        first_select_kernel,
        (shape(index.shape[1] // BLOCK, 2 * CAP, b.shape[1]), shape(*index.shape, dtype=jnp.int32)),
        *args,
        specs=[pl.BlockSpec(memory_space=pltpu.HBM)] * 3,
        scratch_shapes=[pltpu.VMEM(x.shape, x.dtype) for x in (index, b, c)] + [pltpu.SemaphoreType.DMA((3,))],
        flops=10**9,
        size=2**21,
    )


def place_of(index, height):
    eye = lax.broadcasted_iota(jnp.int32, (BLOCK, BLOCK), 0) == lax.broadcasted_iota(jnp.int32, (BLOCK, BLOCK), 1)
    before = lax.broadcasted_iota(jnp.int32, (BLOCK, BLOCK), 1) < lax.broadcasted_iota(jnp.int32, (BLOCK, BLOCK), 0)
    owner = lax.shift_right_logical(index, height.bit_length() - 1)
    owner = jnp.broadcast_to(owner.astype(F32), (BLOCK, BLOCK))
    column = jnp.sum(jnp.where(eye, owner, 0.0), axis=1, keepdims=True)
    slot = jnp.sum(jnp.where((owner == column) & before, 1.0, 0.0), axis=1, keepdims=True)
    return column.astype(jnp.int32), slot.astype(jnp.int32)


def placed_rows(index_ref, column, got, height):
    owners, slots, rank = got.shape
    me = pl.multiple_of(lax.axis_index("row") * BLOCK, BLOCK)
    owner, slot = place_of(index_ref[column : column + 1, pl.ds(me, BLOCK)], height)
    target = owner * slots + column * CAP + slot
    onehot = target == lax.broadcasted_iota(jnp.int32, (BLOCK, owners * slots), 1)
    return pick(jnp.where(onehot, 1.0, 0.0).astype(BF16), got.reshape(owners * slots, rank))


def first_khatri_kernel(height, index_ref, got_ref, out_ref):
    got = got_ref[...]
    rows = [placed_rows(index_ref, column, got, height) for column in range(2)]
    out_ref[...] = rows[0] * rows[1]


def column_scale(got_ref, at, count):
    squares = jnp.sum(got_ref[:, at : min(at + 8, got_ref.shape[1]), :], axis=0)
    return jnp.sqrt(squares[0:1, :] / count + 1e-6)


def second_khatri_kernel(height, index_ref, got_ref, out_ref, scale_ref):
    got = got_ref[...]
    scale = column_scale(got_ref, 2 * CAP, height * got_ref.shape[0])
    scale_ref[...] = jnp.broadcast_to(scale, scale_ref.shape)
    rows = placed_rows(index_ref, 0, got, height) / scale
    out_ref[...] = rows * placed_rows(index_ref, 1, got, height)


GROUP = 4


def invert_block(tiles):
    sub = lax.broadcasted_iota(jnp.int32, (8, 128), 0)
    lane = lax.broadcasted_iota(jnp.int32, (8, 128), 1)
    wide = lambda part: jnp.broadcast_to(part, (8, 128))

    def group(_, tiles):
        tiles = list(tiles)
        for j in range(GROUP):
            t = tiles[j]
            cols = [wide(t[:, 8 * j + k : 8 * j + k + 1]) for k in range(8)]
            in_panel = (lane >= 8 * j) & (lane < 8 * j + 8)
            rows = jnp.where(in_panel, jnp.where(lane == sub + 8 * j, 1.0, 0.0), t)
            for k in range(8):
                inverse = 1.0 / wide(cols[k][k : k + 1, :])
                here = sub == k
                factor = jnp.where(here, 0.0, cols[k])
                row = wide(rows[k : k + 1, :]) * inverse
                rows = jnp.where(here, row, rows - factor * row)
                for m in range(k + 1, 8):
                    entry = wide(cols[m][k : k + 1, :]) * inverse
                    cols[m] = jnp.where(here, entry, cols[m] - factor * entry)
            spread_rows = [wide(rows[k : k + 1, :]) for k in range(8)]
            for i in list(range(j + 1, len(tiles))) + list(range(j)):
                t = tiles[i]
                kept = jnp.where(in_panel, 0.0, t)
                for k in range(8):
                    kept = kept - wide(t[:, 8 * j + k : 8 * j + k + 1]) * spread_rows[k]
                tiles[i] = kept
            tiles[j] = rows
        tiles = [pltpu.roll(t, 128 - 8 * GROUP, 1) for t in tiles]
        return tuple(tiles[GROUP:] + tiles[:GROUP])

    return jnp.concatenate(lax.fori_loop(0, len(tiles) // GROUP, group, tuple(tiles)), axis=0)


def first_inverse_kernel(*refs):
    pieces, (a_ref, w_ref, rest_ref, p_ref, q_ref, r_ref) = refs[:4], refs[4:]
    z, _ = position()
    h = p_ref.shape[0]
    rows, few = h // 4, h // 8
    for step, piece in enumerate(pieces):
        place = quarter(z, -step)
        at = pl.ds(pl.multiple_of(place * rows, rows), rows)
        low = pl.multiple_of(place * few, few)
        p_ref[at, :], r_ref[at, :] = piece[:rows, :h], piece[:rows, h:]
        q_ref[pl.ds(low, few), :], q_ref[pl.ds(low + h // 2, few), :] = piece[rows:, :h], piece[rows:, h:]
    a_ref[...] = invert_block([p_ref[8 * i : 8 * i + 8, :] for i in range(h // 8)])
    w_ref[...] = dot(a_ref[...], q_ref[...])
    rest_ref[...] = r_ref[...] - dot(q_ref[...], w_ref[...], (0, 0))


def second_inverse_kernel(a_ref, w_ref, rest_ref, out_ref):
    h = a_ref.shape[0]
    s = invert_block([rest_ref[8 * i : 8 * i + 8, :] for i in range(h // 8)])
    ws = dot(w_ref[...], s)
    out_ref[h:, h:] = s
    out_ref[:h, h:] = -ws
    out_ref[h:, :h] = -ws.T
    out_ref[:h, :h] = a_ref[...] + dot(ws, w_ref[...], (1, 1))


def join_kernel(place, a, b, c, d, out_ref):
    for step, piece in enumerate((a, b, c, d)):
        at = pl.multiple_of(quarter(place(), -step) * BLOCK, BLOCK)
        out_ref[pl.ds(at, BLOCK), :] = piece[...]


def joined(pieces, place):
    rows, rank = pieces[0].shape
    return call(lambda *refs: join_kernel(place, *refs), shape(4 * rows, rank), *pieces, size=2**20)


LINES = (0, -1, 1, 2)


def split_kernel(fibres_ref, *refs):
    outs, (held, sems) = refs[:8], refs[8:]
    x, y = place_in_row()
    _, _, rows, _ = held.shape
    copies = []
    for n, beside in enumerate(LINES):
        for half in range(2):
            copies.append([])
            for place in range(4):
                at = pl.multiple_of((4 * place + quarter(x - 2 * y + 8, 2 * place + beside)) * BLOCK, BLOCK)
                source = fibres_ref.at[half * rows : (half + 1) * rows, pl.ds(at, BLOCK)]
                target = held.at[n, half, :, place * BLOCK : (place + 1) * BLOCK]
                copies[-1].append(pltpu.make_async_copy(source, target, sems.at[n, half, place]))
                copies[-1][-1].start()
    for n in range(4):
        for half in range(2):
            for copy in copies[2 * n + half]:
                copy.wait()
            mine = slice(half * rows, (half + 1) * rows)
            outs[2 * n][mine, :], outs[2 * n + 1][mine, :] = halves(held[n, half])


def split(fibres):
    rows, samples = fibres.shape
    depth = samples // 4
    return call(
        split_kernel,
        (shape(rows, depth, dtype=BF16),) * 8,
        pltpu.with_memory_space_constraint(fibres, pltpu.HBM),
        specs=[pl.BlockSpec(memory_space=pltpu.HBM)],
        scratch_shapes=[pltpu.VMEM((4, 2, rows // 2, depth), F32), pltpu.SemaphoreType.DMA((4, 2, 4))],
        flops=4 * fibres.size,
        size=8 * fibres.size,
    )


def three_dots(high, low, khatri_high, khatri_low):
    return bf16_dot(high, khatri_high) + (bf16_dot(high, khatri_low) + bf16_dot(low, khatri_high))


def gram_of(high, low):
    t = lambda a, b: lax.dot_general(a, b, (((0,), (0,)), ((), ())), preferred_element_type=F32)
    cross = t(high, low)
    return t(high, high) + (cross + cross.T)


def piece_kernel(high_ref, low_ref, khatri_ref, *refs):
    so_far, (total_ref, gram_ref) = refs[:-2], refs[-2:]
    khatri = halves(khatri_ref[...])
    total, gram = three_dots(high_ref[...], low_ref[...], *khatri), gram_of(*khatri)
    total_ref[...] = total + so_far[0][...] if so_far else total
    gram_ref[...] = gram + so_far[1][...] if so_far else gram


def half_of(high_ref, low_ref, khatri, total_ref, core, out_ref):
    rows = high_ref.shape[0] // 2
    mine = pl.ds(pl.multiple_of(core * rows, rows), rows)
    total = three_dots(high_ref[mine, :], low_ref[mine, :], *khatri) + total_ref[mine, :]
    for place in range(4):
        out_ref[place, :BLOCK, :] = total[place * BLOCK : (place + 1) * BLOCK]


def given_kernel(high_ref, low_ref, khatri_ref, total_ref, gram_ref, out_ref):
    _, core = position()
    khatri = halves(khatri_ref[...])
    half_of(high_ref, low_ref, khatri, total_ref, 1 - core, out_ref)
    gram = gram_of(*khatri) + gram_ref[...]
    h = gram.shape[0] // 2
    rows, few = h // 4, h // 8
    for place in range(4):
        at, low = slice(place * rows, (place + 1) * rows), place * few
        out_ref[place, BLOCK : BLOCK + rows, :h] = gram[at, :h]
        out_ref[place, BLOCK : BLOCK + rows, h:] = gram[h:, h:][at]
        out_ref[place, BLOCK + rows :, :h] = gram[low : low + few, h:]
        out_ref[place, BLOCK + rows :, h:] = gram[h // 2 + low : h // 2 + low + few, h:]


def kept_kernel(high_ref, low_ref, khatri_ref, total_ref, given_ref, out_ref):
    _, core = position()
    half_of(high_ref, low_ref, halves(khatri_ref[...]), total_ref, core, out_ref)
    out_ref[:, BLOCK:, :] = given_ref[:, BLOCK:, :]


def pair_kernel(kept_ref, given_ref, *outs):
    z, _ = position()
    for step, out_ref in enumerate(outs):
        place = quarter(z, step)
        out_ref[...] = kept_ref[place] + given_ref[place]


def quarter_kernel(a, b, c, d, product_ref, gram_ref):
    total = (a[...] + b[...]) + (c[...] + d[...])
    product_ref[...] = total[:BLOCK]
    gram_ref[...] = total[BLOCK:]


def from_z(own):
    got = {step: lax.ppermute(own, "samp", along_z(step)) for step in FAR_FIRST}
    return [own, got[1], got[2], got[3]]


def sums_over_row_group(fibres, block, aside):
    rank = block.shape[1]
    rows, samples = fibres.shape
    depth = samples // 4
    flops = 6 * rows * depth * rank
    near = {step: lax.ppermute(block, "row", in_plane(step, 2 * step)) for step in FAR_FIRST}
    piece = joined([block, near[1], near[2], near[3]], lambda: place_in_row()[1])
    fibres, piece = lax.optimization_barrier((fibres, piece))
    parts = split(fibres)
    moves = {-1: (0, 1), 1: (0, -1), 2: (1, 0)}
    pieces = {beside: lax.ppermute(piece, "row", in_plane(*move)) for beside, move in moves.items()}
    pieces[0] = piece
    state = ()
    for n, beside in enumerate(LINES[:3]):
        high, low = parts[2 * n : 2 * n + 2]
        out = (shape(rows, rank), shape(rank, rank))
        state = call(piece_kernel, out, high, low, pieces[beside], *state, flops=flops, size=2**22)
        if n == 0:
            state, extra = lax.optimization_barrier((state, aside(piece)))
    total, gram = state
    high, low = parts[6:]
    out = shape(4, BLOCK + 3 * rank // 16, rank)
    given = call(given_kernel, out, high, low, pieces[2], total, gram, flops=flops, size=2**21)
    got = lax.ppermute(given, "samp", CORE)
    kept = call(kept_kernel, out, high, low, pieces[2], total, given, flops=flops // 2, size=2**21)
    return kept, got, extra


def summed(fibres, block, aside):
    rank = block.shape[1]
    kept, got, extra = sums_over_row_group(fibres, block, aside)
    rows = kept.shape[1]
    pairs = call(pair_kernel, (shape(rows, rank),) * 4, kept, got, size=2**21)
    parts = [pairs[0]] + [lax.ppermute(pairs[step], "samp", along_z(step)) for step in FAR_FIRST]
    product, gram = call(quarter_kernel, (shape(BLOCK, rank), shape(3 * rank // 16, rank)), *parts, size=2**20)
    h = rank // 2
    first = call(
        first_inverse_kernel,
        (shape(h, h),) * 3,
        *from_z(gram),
        scratch_shapes=[pltpu.VMEM((h, h), F32)] * 3,
        flops=10**11,
        size=2**19,
    )
    first, pieces = lax.optimization_barrier((first, from_z(product)))
    mine = joined(pieces, lambda: position()[0])
    other = lax.ppermute(mine, "samp", CORE)
    inverse = call(second_inverse_kernel, shape(rank, rank), *first, flops=10**11, size=2**19)
    return mine, other, inverse, extra


def solve_into(out_ref, mine_ref, other_ref, inverse_ref):
    _, core = position()
    inverse = halves(inverse_ref[...])
    rows = mine_ref.shape[0]
    for owner, ref in ((core, mine_ref), (1 - core, other_ref)):
        out_ref[pl.ds(pl.multiple_of(owner * rows, rows), rows), :] = three_dots(*halves(ref[...]), *inverse)


def select_kernel(index_ref, c_ref, out_ref, slots_ref):
    select_into(out_ref, 0, slots_of(index_ref, 1, c_ref.shape[0]), c_ref[...])
    slots_ref[...] = slots_of(index_ref, 0, c_ref.shape[0])


def first_solve_kernel(mine_ref, other_ref, inverse_ref, chosen_ref, slots_ref, solved_ref, out_ref):
    solve_into(solved_ref, mine_ref, other_ref, inverse_ref)
    solved = solved_ref[...]
    peers, _, rank = out_ref.shape
    squares = jnp.sum(solved * solved, axis=0, keepdims=True)
    out_ref[:, 2 * CAP :, :] = jnp.broadcast_to(squares[None], (peers, 8, rank))
    out_ref[:, CAP : 2 * CAP, :] = chosen_ref[...]
    select_into(out_ref, 0, slots_ref[...], solved)


def second_solve_kernel(mine_ref, other_ref, inverse_ref, solved_ref, out_ref):
    solve_into(solved_ref, mine_ref, other_ref, inverse_ref)
    solved = solved_ref[...]
    out_ref[...] = jnp.broadcast_to(jnp.sum(solved * solved, axis=0, keepdims=True)[None], out_ref.shape)


def finish_kernel(solved_ref, got_ref, out_ref, scale_ref):
    scale = column_scale(got_ref, 0, solved_ref.shape[0] * got_ref.shape[0])
    scale_ref[...] = jnp.broadcast_to(scale, scale_ref.shape)
    out_ref[...] = solved_ref[...] / scale


def exchange(rows):
    return lax.all_to_all(rows, "row", 0, 0, tiled=True)


def shards(fibres_first, fibres_second, index_first, index_second, factor_b, factor_c):
    height, rank = factor_b.shape
    peers = index_first.shape[0] // BLOCK
    first, second = index_first.T, index_second.T

    sent, first = first_select(first, factor_b, factor_c)
    got = exchange(sent)
    block = call(lambda *refs: first_khatri_kernel(height, *refs), shape(BLOCK, rank), first, got, flops=10**8, size=2**22)

    def choose(piece):
        index, rows, _ = lax.optimization_barrier((second, factor_c, piece))
        out = (shape(peers, CAP, rank), shape(peers * CAP, height, dtype=BF16))
        return call(select_kernel, out, index, rows, flops=10**9, size=2**21)

    mine, other, inverse, chosen = summed(fibres_first, block, choose)
    solved, sent = call(
        first_solve_kernel,
        (shape(height, rank), shape(peers, 2 * CAP + 8, rank)),
        mine,
        other,
        inverse,
        *chosen,
        flops=10**9,
        size=2**21,
    )
    block, scale = call(
        lambda *refs: second_khatri_kernel(height, *refs),
        (shape(BLOCK, rank), shape(8, rank)),
        second,
        exchange(sent),
        flops=10**8,
        size=2**22,
    )

    def normalise(piece):
        rows, _ = lax.optimization_barrier((solved, piece))
        return rows / scale[:1]

    mine, other, inverse, factor_a = summed(fibres_second, block, normalise)
    solved, sent = call(
        second_solve_kernel,
        (shape(height, rank), shape(peers, 1, rank)),
        mine,
        other,
        inverse,
        flops=10**9,
        size=2**21,
    )
    factor_b_new, weights = call(finish_kernel, (shape(height, rank), shape(8, rank)), solved, exchange(sent), size=2**21)
    return (factor_a, factor_b_new, weights[0])


def solution(mesh):
    placed = (P("row", "samp"), P("row", "samp"), P("samp", None), P("samp", None), P("row", None), P("row", None))
    return jax.shard_map(
        shards,
        mesh=mesh,
        in_specs=placed,
        out_specs=(P("row", None), P("row", None), P()),
        check_vma=False,
    )
```

```python
import jax
import jax.numpy as jnp
from jax import lax
from jax.experimental import pallas as pl
from jax.experimental.pallas import tpu as pltpu
from jax.sharding import PartitionSpec as P

F32, BF16 = jnp.float32, jnp.bfloat16
CAP = 16
BLOCK = 128
HIGHEST = lax.Precision.HIGHEST
VMEM = pl.BlockSpec(memory_space=pltpu.VMEM)
CORE = [(i, i ^ 1) for i in range(8)]
FAR_FIRST = (2, 1, 3)


def in_plane(down, right):
    return [(row, (row // 4 + down) % 4 * 4 + (row + right) % 4) for row in range(16)]


def along_z(step):
    return [(2 * z + c, (2 * z + 2 * step) % 8 + c) for z in range(4) for c in range(2)]


def call(kernel, out, *args, flops=0, size=0, specs=None, **kwargs):
    return pl.pallas_call(
        kernel,
        out_shape=out,
        in_specs=specs or [VMEM] * len(args),
        out_specs=jax.tree.map(lambda _: VMEM, out),
        cost_estimate=pl.CostEstimate(flops=flops, bytes_accessed=size, transcendentals=0),
        compiler_params=pltpu.CompilerParams(vmem_limit_bytes=32 * 2**20),
        **kwargs,
    )(*args)


def shape(*dims, dtype=F32):
    return jax.ShapeDtypeStruct(dims, dtype)


def dot(a, b, dims=(1, 0)):
    return lax.dot_general(a, b, (((dims[0],), (dims[1],)), ((), ())), precision=HIGHEST, preferred_element_type=F32)


def bf16_dot(a, b):
    return jnp.dot(a, b, preferred_element_type=F32)


def halves(x):
    high = x.astype(BF16)
    return high, (x - high.astype(F32)).astype(BF16)


def pick(onehot, x):
    high, low = halves(x)
    return bf16_dot(onehot, high) + bf16_dot(onehot, low)


def position():
    samp = lax.axis_index("samp")
    return lax.shift_right_logical(samp, 1), lax.bitwise_and(samp, 1)


def quarter(place, step):
    return lax.bitwise_and(place + step + 4, 3)


def place_in_row():
    row = lax.axis_index("row")
    return lax.bitwise_and(row, 3), lax.shift_right_logical(row, 2)


def slots_of(index_ref, column, height):
    blocks = index_ref.shape[1] // BLOCK
    wanted = [index_ref[column : column + 1, t * BLOCK : (t + 1) * BLOCK] for t in range(blocks)]
    local = jnp.concatenate(wanted, axis=0) - lax.axis_index("row") * height
    inside = (local >= 0) & (local < height)
    before = lax.broadcasted_iota(jnp.int32, (BLOCK, BLOCK), 0) < lax.broadcasted_iota(jnp.int32, (BLOCK, BLOCK), 1)
    slot = bf16_dot(jnp.where(inside, 1.0, 0.0).astype(BF16), jnp.where(before, 1.0, 0.0).astype(BF16))
    slot = jnp.where(inside, slot.astype(jnp.int32), -1)
    which = lax.broadcasted_iota(jnp.int32, (blocks, CAP, BLOCK), 1)
    wanted = jnp.where(slot[:, None, :] == which, local[:, None, :] + 1, 0)
    row = jnp.sum(wanted.astype(F32), axis=2, keepdims=True).astype(jnp.int32).reshape(blocks * CAP, 1) - 1
    return jnp.where(row == lax.broadcasted_iota(jnp.int32, (blocks * CAP, height), 1), 1.0, 0.0).astype(BF16)


def select_into(out_ref, part, onehot, rows):
    picked = pick(onehot, rows)
    out_ref[:, part * CAP : (part + 1) * CAP, :] = picked.reshape(-1, CAP, picked.shape[-1])


def first_select_kernel(index_hbm, b_hbm, c_hbm, out_ref, index_out, index_ref, b_ref, c_ref, sems):
    pairs = ((index_hbm, index_ref), (b_hbm, b_ref), (c_hbm, c_ref))
    copies = [pltpu.make_async_copy(src, dst, sems.at[n]) for n, (src, dst) in enumerate(pairs)]
    for copy in copies:
        copy.start()
    copies[0].wait()
    index_out[...] = index_ref[...]
    onehots = [slots_of(index_ref, column, b_ref.shape[0]) for column in range(2)]
    for column, rows in enumerate((b_ref, c_ref)):
        copies[column + 1].wait()
        select_into(out_ref, column, onehots[column], rows[...])


def first_select(index, b, c):
    args = [pltpu.with_memory_space_constraint(x, pltpu.HBM) for x in (index, b, c)]
    return call(
        first_select_kernel,
        (shape(index.shape[1] // BLOCK, 2 * CAP, b.shape[1]), shape(*index.shape, dtype=jnp.int32)),
        *args,
        specs=[pl.BlockSpec(memory_space=pltpu.HBM)] * 3,
        scratch_shapes=[pltpu.VMEM(x.shape, x.dtype) for x in (index, b, c)] + [pltpu.SemaphoreType.DMA((3,))],
        flops=10**9,
        size=2**21,
    )


def place_of(index, height):
    eye = lax.broadcasted_iota(jnp.int32, (BLOCK, BLOCK), 0) == lax.broadcasted_iota(jnp.int32, (BLOCK, BLOCK), 1)
    before = lax.broadcasted_iota(jnp.int32, (BLOCK, BLOCK), 1) < lax.broadcasted_iota(jnp.int32, (BLOCK, BLOCK), 0)
    owner = lax.shift_right_logical(index, height.bit_length() - 1)
    owner = jnp.broadcast_to(owner.astype(F32), (BLOCK, BLOCK))
    column = jnp.sum(jnp.where(eye, owner, 0.0), axis=1, keepdims=True)
    slot = jnp.sum(jnp.where((owner == column) & before, 1.0, 0.0), axis=1, keepdims=True)
    return column.astype(jnp.int32), slot.astype(jnp.int32)


def placed_rows(index_ref, column, got, height):
    owners, slots, rank = got.shape
    me = pl.multiple_of(lax.axis_index("row") * BLOCK, BLOCK)
    owner, slot = place_of(index_ref[column : column + 1, pl.ds(me, BLOCK)], height)
    target = owner * slots + column * CAP + slot
    onehot = target == lax.broadcasted_iota(jnp.int32, (BLOCK, owners * slots), 1)
    return pick(jnp.where(onehot, 1.0, 0.0).astype(BF16), got.reshape(owners * slots, rank))


def first_khatri_kernel(height, index_ref, got_ref, out_ref):
    got = got_ref[...]
    rows = [placed_rows(index_ref, column, got, height) for column in range(2)]
    out_ref[...] = rows[0] * rows[1]


def column_scale(got_ref, at, count):
    squares = jnp.sum(got_ref[:, at : min(at + 8, got_ref.shape[1]), :], axis=0)
    return jnp.sqrt(squares[0:1, :] / count + 1e-6)


def second_khatri_kernel(height, index_ref, got_ref, out_ref, scale_ref):
    got = got_ref[...]
    scale = column_scale(got_ref, 2 * CAP, height * got_ref.shape[0])
    scale_ref[...] = jnp.broadcast_to(scale, scale_ref.shape)
    rows = placed_rows(index_ref, 0, got, height) * (1.0 / scale)
    out_ref[...] = rows * placed_rows(index_ref, 1, got, height)


GROUP = 4


def invert_block(tiles):
    sub = lax.broadcasted_iota(jnp.int32, (8, 128), 0)
    lane = lax.broadcasted_iota(jnp.int32, (8, 128), 1)
    wide = lambda part: jnp.broadcast_to(part, (8, 128))

    def group(_, tiles):
        tiles = list(tiles)
        for j in range(GROUP):
            t = tiles[j]
            cols = [wide(t[:, 8 * j + k : 8 * j + k + 1]) for k in range(8)]
            in_panel = (lane >= 8 * j) & (lane < 8 * j + 8)
            rows = jnp.where(in_panel, jnp.where(lane == sub + 8 * j, 1.0, 0.0), t)
            for k in range(8):
                inverse = 1.0 / wide(cols[k][k : k + 1, :])
                here = sub == k
                factor = jnp.where(here, 0.0, cols[k])
                row = wide(rows[k : k + 1, :]) * inverse
                rows = jnp.where(here, row, rows - factor * row)
                for m in range(k + 1, 8):
                    entry = wide(cols[m][k : k + 1, :]) * inverse
                    cols[m] = jnp.where(here, entry, cols[m] - factor * entry)
            spread_rows = [wide(rows[k : k + 1, :]) for k in range(8)]
            for i in list(range(j + 1, len(tiles))) + list(range(j)):
                t = tiles[i]
                kept = jnp.where(in_panel, 0.0, t)
                for k in range(8):
                    kept = kept - wide(t[:, 8 * j + k : 8 * j + k + 1]) * spread_rows[k]
                tiles[i] = kept
            tiles[j] = rows
        tiles = [pltpu.roll(t, 128 - 8 * GROUP, 1) for t in tiles]
        return tuple(tiles[GROUP:] + tiles[:GROUP])

    return jnp.concatenate(lax.fori_loop(0, len(tiles) // GROUP, group, tuple(tiles)), axis=0)


def first_inverse_kernel(*refs):
    pieces, (a_ref, w_ref, rest_ref, p_ref, q_ref, r_ref) = refs[:4], refs[4:]
    z, _ = position()
    h = p_ref.shape[0]
    rows, few = h // 4, h // 8
    for step, piece in enumerate(pieces):
        place = quarter(z, -step)
        at = pl.ds(pl.multiple_of(place * rows, rows), rows)
        low = pl.multiple_of(place * few, few)
        p_ref[at, :], r_ref[at, :] = piece[:rows, :h], piece[:rows, h:]
        q_ref[pl.ds(low, few), :], q_ref[pl.ds(low + h // 2, few), :] = piece[rows:, :h], piece[rows:, h:]
    a_ref[...] = invert_block([p_ref[8 * i : 8 * i + 8, :] for i in range(h // 8)])
    w_ref[...] = dot(a_ref[...], q_ref[...])
    rest_ref[...] = r_ref[...] - dot(q_ref[...], w_ref[...], (0, 0))


def second_inverse_kernel(a_ref, w_ref, rest_ref, out_ref):
    h = a_ref.shape[0]
    s = invert_block([rest_ref[8 * i : 8 * i + 8, :] for i in range(h // 8)])
    ws = dot(w_ref[...], s)
    out_ref[h:, h:] = s
    out_ref[:h, h:] = -ws
    out_ref[h:, :h] = -ws.T
    out_ref[:h, :h] = a_ref[...] + dot(ws, w_ref[...], (1, 1))


def join_kernel(place, a, b, c, d, out_ref):
    for step, piece in enumerate((a, b, c, d)):
        at = pl.multiple_of(quarter(place(), -step) * BLOCK, BLOCK)
        out_ref[pl.ds(at, BLOCK), :] = piece[...]


def joined(pieces, place):
    rows, rank = pieces[0].shape
    return call(lambda *refs: join_kernel(place, *refs), shape(4 * rows, rank), *pieces, size=2**20)


LINES = (0, -1, 1, 2)


def split_kernel(fibres_ref, *refs):
    outs, (held, sems) = refs[:8], refs[8:]
    x, y = place_in_row()
    _, _, rows, _ = held.shape
    copies = []
    for n, beside in enumerate(LINES):
        for half in range(2):
            copies.append([])
            for place in range(4):
                at = pl.multiple_of((4 * place + quarter(x - 2 * y + 8, 2 * place + beside)) * BLOCK, BLOCK)
                source = fibres_ref.at[half * rows : (half + 1) * rows, pl.ds(at, BLOCK)]
                target = held.at[n, half, :, place * BLOCK : (place + 1) * BLOCK]
                copies[-1].append(pltpu.make_async_copy(source, target, sems.at[n, half, place]))
                copies[-1][-1].start()
    for n in range(4):
        for half in range(2):
            for copy in copies[2 * n + half]:
                copy.wait()
            mine = slice(half * rows, (half + 1) * rows)
            outs[2 * n][mine, :], outs[2 * n + 1][mine, :] = halves(held[n, half])


def split(fibres):
    rows, samples = fibres.shape
    depth = samples // 4
    return call(
        split_kernel,
        (shape(rows, depth, dtype=BF16),) * 8,
        pltpu.with_memory_space_constraint(fibres, pltpu.HBM),
        specs=[pl.BlockSpec(memory_space=pltpu.HBM)],
        scratch_shapes=[pltpu.VMEM((4, 2, rows // 2, depth), F32), pltpu.SemaphoreType.DMA((4, 2, 4))],
        flops=4 * fibres.size,
        size=8 * fibres.size,
    )


def three_dots(high, low, khatri_high, khatri_low):
    return bf16_dot(high, khatri_high) + (bf16_dot(high, khatri_low) + bf16_dot(low, khatri_high))


def gram_of(high, low):
    t = lambda a, b: lax.dot_general(a, b, (((0,), (0,)), ((), ())), preferred_element_type=F32)
    cross = t(high, low)
    return t(high, high) + (cross + cross.T)


def half_of(ref, core):
    rows = ref.shape[0] // 2
    return ref[pl.ds(pl.multiple_of(core * rows, rows), rows), :]


def piece_kernel(high_ref, low_ref, khatri_ref, *refs):
    so_far, (total_ref, gram_ref) = refs[:-2], refs[-2:]
    _, core = position()
    khatri = halves(khatri_ref[...])
    total = three_dots(half_of(high_ref, 1 - core), half_of(low_ref, 1 - core), *khatri)
    gram = gram_of(*khatri)
    total_ref[...] = total + so_far[0][...] if so_far else total
    gram_ref[...] = gram + so_far[1][...] if so_far else gram


def by_quarters(out_ref, total):
    for place in range(4):
        out_ref[place, :BLOCK, :] = total[place * BLOCK : (place + 1) * BLOCK]


def given_kernel(high_ref, low_ref, khatri_ref, total_ref, gram_ref, out_ref):
    _, core = position()
    khatri = halves(khatri_ref[...])
    by_quarters(out_ref, three_dots(half_of(high_ref, 1 - core), half_of(low_ref, 1 - core), *khatri) + total_ref[...])
    gram = gram_of(*khatri) + gram_ref[...]
    h = gram.shape[0] // 2
    rows, few = h // 4, h // 8
    for place in range(4):
        at, low = slice(place * rows, (place + 1) * rows), place * few
        out_ref[place, BLOCK : BLOCK + rows, :h] = gram[at, :h]
        out_ref[place, BLOCK : BLOCK + rows, h:] = gram[h:, h:][at]
        out_ref[place, BLOCK + rows :, :h] = gram[low : low + few, h:]
        out_ref[place, BLOCK + rows :, h:] = gram[h // 2 + low : h // 2 + low + few, h:]


def kept_kernel(*refs):
    parts, pieces, (given_ref, out_ref) = refs[:8], refs[8:12], refs[12:]
    _, core = position()
    total = None
    for n, khatri_ref in enumerate(pieces):
        part = three_dots(half_of(parts[2 * n], core), half_of(parts[2 * n + 1], core), *halves(khatri_ref[...]))
        total = part if total is None else total + part
    by_quarters(out_ref, total)
    out_ref[:, BLOCK:, :] = given_ref[:, BLOCK:, :]


def pair_kernel(kept_ref, given_ref, *outs):
    z, _ = position()
    for step, out_ref in enumerate(outs):
        place = quarter(z, step)
        out_ref[...] = kept_ref[place] + given_ref[place]


def quarter_kernel(a, b, c, d, product_ref, gram_ref):
    total = (a[...] + b[...]) + (c[...] + d[...])
    product_ref[...] = total[:BLOCK]
    gram_ref[...] = total[BLOCK:]


def from_z(own):
    got = {step: lax.ppermute(own, "samp", along_z(step)) for step in FAR_FIRST}
    return [own, got[1], got[2], got[3]]


def sums_over_row_group(fibres, block, aside):
    rank = block.shape[1]
    rows, samples = fibres.shape
    depth = samples // 4
    flops = 6 * rows * depth * rank
    near = {step: lax.ppermute(block, "row", in_plane(step, 2 * step)) for step in FAR_FIRST}
    piece = joined([block, near[1], near[2], near[3]], lambda: place_in_row()[1])
    fibres, piece = lax.optimization_barrier((fibres, piece))
    parts = split(fibres)
    moves = {-1: (0, 1), 1: (0, -1), 2: (1, 0)}
    pieces = {beside: lax.ppermute(piece, "row", in_plane(*move)) for beside, move in moves.items()}
    pieces[0] = piece
    state = ()
    for n, beside in enumerate(LINES[:3]):
        high, low = parts[2 * n : 2 * n + 2]
        out = (shape(rows // 2, rank), shape(rank, rank))
        state = call(piece_kernel, out, high, low, pieces[beside], *state, flops=flops // 2, size=2**21)
        if n == 0:
            state, extra = lax.optimization_barrier((state, aside(piece)))
    total, gram = state
    high, low = parts[6:]
    out = shape(4, BLOCK + 3 * rank // 16, rank)
    given = call(given_kernel, out, high, low, pieces[2], total, gram, flops=flops, size=2**21)
    got = lax.ppermute(given, "samp", CORE)
    kept = call(kept_kernel, out, *parts, *[pieces[beside] for beside in LINES], given, flops=2 * flops, size=2**23)
    return kept, got, extra


def summed(fibres, block, aside):
    rank = block.shape[1]
    kept, got, extra = sums_over_row_group(fibres, block, aside)
    pairs = call(pair_kernel, (shape(*kept.shape[1:]),) * 4, kept, got, size=2**21)
    parts = [pairs[0]] + [lax.ppermute(pairs[step], "samp", along_z(step)) for step in FAR_FIRST]
    product, gram = call(quarter_kernel, (shape(BLOCK, rank), shape(3 * rank // 16, rank)), *parts, size=2**20)
    h = rank // 2
    first = call(
        first_inverse_kernel,
        (shape(h, h),) * 3,
        *from_z(gram),
        scratch_shapes=[pltpu.VMEM((h, h), F32)] * 3,
        flops=10**11,
        size=2**19,
    )
    first, pieces = lax.optimization_barrier((first, from_z(product)))
    mine = joined(pieces, lambda: position()[0])
    other = lax.ppermute(mine, "samp", CORE)
    inverse = call(second_inverse_kernel, shape(rank, rank), *first, flops=10**11, size=2**19)
    return mine, other, inverse, extra


def solve_into(out_ref, mine_ref, other_ref, inverse_ref):
    _, core = position()
    inverse = halves(inverse_ref[...])
    rows = mine_ref.shape[0]
    for owner, ref in ((core, mine_ref), (1 - core, other_ref)):
        out_ref[pl.ds(pl.multiple_of(owner * rows, rows), rows), :] = three_dots(*halves(ref[...]), *inverse)


def select_kernel(index_ref, c_ref, out_ref, slots_ref):
    select_into(out_ref, 0, slots_of(index_ref, 1, c_ref.shape[0]), c_ref[...])
    slots_ref[...] = slots_of(index_ref, 0, c_ref.shape[0])


def first_solve_kernel(mine_ref, other_ref, inverse_ref, chosen_ref, slots_ref, solved_ref, out_ref):
    solve_into(solved_ref, mine_ref, other_ref, inverse_ref)
    solved = solved_ref[...]
    peers, _, rank = out_ref.shape
    squares = jnp.sum(solved * solved, axis=0, keepdims=True)
    out_ref[:, 2 * CAP :, :] = jnp.broadcast_to(squares[None], (peers, 8, rank))
    out_ref[:, CAP : 2 * CAP, :] = chosen_ref[...]
    select_into(out_ref, 0, slots_ref[...], solved)


def second_solve_kernel(mine_ref, other_ref, inverse_ref, solved_ref, out_ref):
    solve_into(solved_ref, mine_ref, other_ref, inverse_ref)
    solved = solved_ref[...]
    out_ref[...] = jnp.broadcast_to(jnp.sum(solved * solved, axis=0, keepdims=True)[None], out_ref.shape)


def finish_kernel(solved_ref, got_ref, out_ref, scale_ref):
    scale = column_scale(got_ref, 0, solved_ref.shape[0] * got_ref.shape[0])
    scale_ref[...] = scale
    out_ref[...] = solved_ref[...] * (1.0 / scale)


def exchange(rows):
    return lax.all_to_all(rows, "row", 0, 0, tiled=True)


def shards(fibres_first, fibres_second, index_first, index_second, factor_b, factor_c):
    height, rank = factor_b.shape
    peers = index_first.shape[0] // BLOCK
    first, second = index_first.T, index_second.T

    sent, first = first_select(first, factor_b, factor_c)
    got = exchange(sent)
    block = call(lambda *refs: first_khatri_kernel(height, *refs), shape(BLOCK, rank), first, got, flops=10**8, size=2**22)

    def choose(piece):
        index, rows, _ = lax.optimization_barrier((second, factor_c, piece))
        out = (shape(peers, CAP, rank), shape(peers * CAP, height, dtype=BF16))
        return call(select_kernel, out, index, rows, flops=10**9, size=2**21)

    mine, other, inverse, chosen = summed(fibres_first, block, choose)
    solved, sent = call(
        first_solve_kernel,
        (shape(height, rank), shape(peers, 2 * CAP + 8, rank)),
        mine,
        other,
        inverse,
        *chosen,
        flops=10**9,
        size=2**21,
    )
    block, scale = call(
        lambda *refs: second_khatri_kernel(height, *refs),
        (shape(BLOCK, rank), shape(8, rank)),
        second,
        exchange(sent),
        flops=10**8,
        size=2**22,
    )

    def normalise(piece):
        rows, _ = lax.optimization_barrier((solved, piece))
        return rows / scale[:1]

    mine, other, inverse, factor_a = summed(fibres_second, block, normalise)
    solved, sent = call(
        second_solve_kernel,
        (shape(height, rank), shape(peers, 1, rank)),
        mine,
        other,
        inverse,
        flops=10**9,
        size=2**21,
    )
    factor_b_new, weights = call(finish_kernel, (shape(height, rank), shape(1, rank)), solved, exchange(sent), size=2**21)
    return (factor_a, factor_b_new, weights.reshape(rank))


def solution(mesh):
    placed = (P("row", "samp"), P("row", "samp"), P("samp", None), P("samp", None), P("row", None), P("row", None))
    return jax.shard_map(
        shards,
        mesh=mesh,
        in_specs=placed,
        out_specs=(P("row", None), P("row", None), P()),
        check_vma=False,
    )
```

```python
import jax
import jax.numpy as jnp
from jax import lax
from jax.experimental import pallas as pl
from jax.experimental.pallas import tpu as pltpu
from jax.sharding import PartitionSpec as P

F32, BF16 = jnp.float32, jnp.bfloat16
CAP = 16
BLOCK = 128
HIGHEST = lax.Precision.HIGHEST
VMEM = pl.BlockSpec(memory_space=pltpu.VMEM)
CORE = [(i, i ^ 1) for i in range(8)]
FAR_FIRST = (2, 1, 3)


def in_plane(down, right):
    return [(row, (row // 4 + down) % 4 * 4 + (row + right) % 4) for row in range(16)]


def along_z(step):
    return [(2 * z + c, (2 * z + 2 * step) % 8 + c) for z in range(4) for c in range(2)]


def call(kernel, out, *args, flops=0, size=0, specs=None, **kwargs):
    return pl.pallas_call(
        kernel,
        out_shape=out,
        in_specs=specs or [VMEM] * len(args),
        out_specs=jax.tree.map(lambda _: VMEM, out),
        cost_estimate=pl.CostEstimate(flops=flops, bytes_accessed=size, transcendentals=0),
        compiler_params=pltpu.CompilerParams(vmem_limit_bytes=32 * 2**20),
        **kwargs,
    )(*args)


def shape(*dims, dtype=F32):
    return jax.ShapeDtypeStruct(dims, dtype)


def dot(a, b, dims=(1, 0)):
    return lax.dot_general(a, b, (((dims[0],), (dims[1],)), ((), ())), precision=HIGHEST, preferred_element_type=F32)


def bf16_dot(a, b):
    return jnp.dot(a, b, preferred_element_type=F32)


def halves(x):
    high = x.astype(BF16)
    return high, (x - high.astype(F32)).astype(BF16)


def pick(onehot, x):
    high, low = halves(x)
    return bf16_dot(onehot, high) + bf16_dot(onehot, low)


def position():
    samp = lax.axis_index("samp")
    return lax.shift_right_logical(samp, 1), lax.bitwise_and(samp, 1)


def quarter(place, step):
    return lax.bitwise_and(place + step + 4, 3)


def place_in_row():
    row = lax.axis_index("row")
    return lax.bitwise_and(row, 3), lax.shift_right_logical(row, 2)


def slots_of(index_ref, column, height):
    blocks = index_ref.shape[1] // BLOCK
    wanted = [index_ref[column : column + 1, t * BLOCK : (t + 1) * BLOCK] for t in range(blocks)]
    local = jnp.concatenate(wanted, axis=0) - lax.axis_index("row") * height
    inside = (local >= 0) & (local < height)
    before = lax.broadcasted_iota(jnp.int32, (BLOCK, BLOCK), 0) < lax.broadcasted_iota(jnp.int32, (BLOCK, BLOCK), 1)
    slot = bf16_dot(jnp.where(inside, 1.0, 0.0).astype(BF16), jnp.where(before, 1.0, 0.0).astype(BF16))
    slot = jnp.where(inside, slot.astype(jnp.int32), -1)
    which = lax.broadcasted_iota(jnp.int32, (blocks, CAP, BLOCK), 1)
    wanted = jnp.where(slot[:, None, :] == which, local[:, None, :] + 1, 0)
    row = jnp.sum(wanted.astype(F32), axis=2, keepdims=True).astype(jnp.int32).reshape(blocks * CAP, 1) - 1
    return jnp.where(row == lax.broadcasted_iota(jnp.int32, (blocks * CAP, height), 1), 1.0, 0.0).astype(BF16)


def select_into(out_ref, part, onehot, rows):
    picked = pick(onehot, rows)
    out_ref[:, part * CAP : (part + 1) * CAP, :] = picked.reshape(-1, CAP, picked.shape[-1])


def first_select_kernel(index_hbm, b_hbm, c_hbm, out_ref, index_out, index_ref, b_ref, c_ref, sems):
    pairs = ((index_hbm, index_ref), (b_hbm, b_ref), (c_hbm, c_ref))
    copies = [pltpu.make_async_copy(src, dst, sems.at[n]) for n, (src, dst) in enumerate(pairs)]
    for copy in copies:
        copy.start()
    copies[0].wait()
    index_out[...] = index_ref[...]
    onehots = [slots_of(index_ref, column, b_ref.shape[0]) for column in range(2)]
    for column, rows in enumerate((b_ref, c_ref)):
        copies[column + 1].wait()
        select_into(out_ref, column, onehots[column], rows[...])


def first_select(index, b, c):
    args = [pltpu.with_memory_space_constraint(x, pltpu.HBM) for x in (index, b, c)]
    return call(
        first_select_kernel,
        (shape(index.shape[1] // BLOCK, 2 * CAP, b.shape[1]), shape(*index.shape, dtype=jnp.int32)),
        *args,
        specs=[pl.BlockSpec(memory_space=pltpu.HBM)] * 3,
        scratch_shapes=[pltpu.VMEM(x.shape, x.dtype) for x in (index, b, c)] + [pltpu.SemaphoreType.DMA((3,))],
        flops=10**9,
        size=2**21,
    )


def place_of(index, height):
    eye = lax.broadcasted_iota(jnp.int32, (BLOCK, BLOCK), 0) == lax.broadcasted_iota(jnp.int32, (BLOCK, BLOCK), 1)
    before = lax.broadcasted_iota(jnp.int32, (BLOCK, BLOCK), 1) < lax.broadcasted_iota(jnp.int32, (BLOCK, BLOCK), 0)
    owner = lax.shift_right_logical(index, height.bit_length() - 1)
    owner = jnp.broadcast_to(owner.astype(F32), (BLOCK, BLOCK))
    column = jnp.sum(jnp.where(eye, owner, 0.0), axis=1, keepdims=True)
    slot = jnp.sum(jnp.where((owner == column) & before, 1.0, 0.0), axis=1, keepdims=True)
    return column.astype(jnp.int32), slot.astype(jnp.int32)


def placed_rows(index_ref, column, got, height):
    owners, slots, rank = got.shape
    me = pl.multiple_of(lax.axis_index("row") * BLOCK, BLOCK)
    owner, slot = place_of(index_ref[column : column + 1, pl.ds(me, BLOCK)], height)
    target = owner * slots + column * CAP + slot
    onehot = target == lax.broadcasted_iota(jnp.int32, (BLOCK, owners * slots), 1)
    return pick(jnp.where(onehot, 1.0, 0.0).astype(BF16), got.reshape(owners * slots, rank))


def first_khatri_kernel(height, index_ref, got_ref, out_ref):
    got = got_ref[...]
    rows = [placed_rows(index_ref, column, got, height) for column in range(2)]
    out_ref[...] = rows[0] * rows[1]


def column_scale(got_ref, at, count):
    squares = jnp.sum(got_ref[:, at : min(at + 8, got_ref.shape[1]), :], axis=0)
    return jnp.sqrt(squares[0:1, :] / count + 1e-6)


def second_khatri_kernel(height, index_ref, got_ref, out_ref, scale_ref):
    got = got_ref[...]
    scale = column_scale(got_ref, 2 * CAP, height * got_ref.shape[0])
    scale_ref[...] = jnp.broadcast_to(scale, scale_ref.shape)
    rows = placed_rows(index_ref, 0, got, height) * (1.0 / scale)
    out_ref[...] = rows * placed_rows(index_ref, 1, got, height)


GROUP = 8


def invert_block(tiles):
    sub = lax.broadcasted_iota(jnp.int32, (8, 128), 0)
    lane = lax.broadcasted_iota(jnp.int32, (8, 128), 1)
    wide = lambda part: jnp.broadcast_to(part, (8, 128))

    def group(_, tiles):
        tiles = list(tiles)
        for j in range(GROUP):
            t = tiles[j]
            cols = [wide(t[:, 8 * j + k : 8 * j + k + 1]) for k in range(8)]
            in_panel = (lane >= 8 * j) & (lane < 8 * j + 8)
            rows = jnp.where(in_panel, jnp.where(lane == sub + 8 * j, 1.0, 0.0), t)
            for k in range(8):
                inverse = 1.0 / wide(cols[k][k : k + 1, :])
                here = sub == k
                factor = jnp.where(here, 0.0, cols[k])
                row = wide(rows[k : k + 1, :]) * inverse
                rows = jnp.where(here, row, rows - factor * row)
                for m in range(k + 1, 8):
                    entry = wide(cols[m][k : k + 1, :]) * inverse
                    cols[m] = jnp.where(here, entry, cols[m] - factor * entry)
            spread_rows = [wide(rows[k : k + 1, :]) for k in range(8)]
            for i in list(range(j + 1, len(tiles))) + list(range(j)):
                t = tiles[i]
                kept = jnp.where(in_panel, 0.0, t)
                for k in range(8):
                    kept = kept - wide(t[:, 8 * j + k : 8 * j + k + 1]) * spread_rows[k]
                tiles[i] = kept
            tiles[j] = rows
        tiles = [pltpu.roll(t, 128 - 8 * GROUP, 1) for t in tiles]
        return tuple(tiles[GROUP:] + tiles[:GROUP])

    return jnp.concatenate(lax.fori_loop(0, len(tiles) // GROUP, group, tuple(tiles)), axis=0)


def first_inverse_kernel(*refs):
    pieces, (a_ref, w_ref, rest_ref, p_ref, q_ref, r_ref) = refs[:4], refs[4:]
    z, _ = position()
    h = p_ref.shape[0]
    rows, few = h // 4, h // 8
    for step, piece in enumerate(pieces):
        place = quarter(z, -step)
        at = pl.ds(pl.multiple_of(place * rows, rows), rows)
        low = pl.multiple_of(place * few, few)
        p_ref[at, :], r_ref[at, :] = piece[:rows, :h], piece[:rows, h:]
        q_ref[pl.ds(low, few), :], q_ref[pl.ds(low + h // 2, few), :] = piece[rows:, :h], piece[rows:, h:]
    a_ref[...] = invert_block([p_ref[8 * i : 8 * i + 8, :] for i in range(h // 8)])
    w_ref[...] = dot(a_ref[...], q_ref[...])
    rest_ref[...] = r_ref[...] - dot(q_ref[...], w_ref[...], (0, 0))


def second_inverse_kernel(a_ref, w_ref, rest_ref, out_ref):
    h = a_ref.shape[0]
    s = invert_block([rest_ref[8 * i : 8 * i + 8, :] for i in range(h // 8)])
    ws = dot(w_ref[...], s)
    out_ref[h:, h:] = s
    out_ref[:h, h:] = -ws
    out_ref[h:, :h] = -ws.T
    out_ref[:h, :h] = a_ref[...] + dot(ws, w_ref[...], (1, 1))


def join_kernel(place, a, b, c, d, out_ref):
    for step, piece in enumerate((a, b, c, d)):
        at = pl.multiple_of(quarter(place(), -step) * BLOCK, BLOCK)
        out_ref[pl.ds(at, BLOCK), :] = piece[...]


def joined(pieces, place):
    rows, rank = pieces[0].shape
    return call(lambda *refs: join_kernel(place, *refs), shape(4 * rows, rank), *pieces, size=2**20)


LINES = (0, -1, 1, 2)


def split_kernel(fibres_ref, *refs):
    outs, (held, sems) = refs[:8], refs[8:]
    x, y = place_in_row()
    _, _, rows, _ = held.shape
    copies = []
    for n, beside in enumerate(LINES):
        for half in range(2):
            copies.append([])
            for place in range(4):
                at = pl.multiple_of((4 * place + quarter(x - 2 * y + 8, 2 * place + beside)) * BLOCK, BLOCK)
                source = fibres_ref.at[half * rows : (half + 1) * rows, pl.ds(at, BLOCK)]
                target = held.at[n, half, :, place * BLOCK : (place + 1) * BLOCK]
                copies[-1].append(pltpu.make_async_copy(source, target, sems.at[n, half, place]))
                copies[-1][-1].start()
    for n in range(4):
        for half in range(2):
            for copy in copies[2 * n + half]:
                copy.wait()
            mine = slice(half * rows, (half + 1) * rows)
            outs[2 * n][mine, :], outs[2 * n + 1][mine, :] = halves(held[n, half])


def split(fibres):
    rows, samples = fibres.shape
    depth = samples // 4
    return call(
        split_kernel,
        (shape(rows, depth, dtype=BF16),) * 8,
        pltpu.with_memory_space_constraint(fibres, pltpu.HBM),
        specs=[pl.BlockSpec(memory_space=pltpu.HBM)],
        scratch_shapes=[pltpu.VMEM((4, 2, rows // 2, depth), F32), pltpu.SemaphoreType.DMA((4, 2, 4))],
        flops=4 * fibres.size,
        size=8 * fibres.size,
    )


def three_dots(high, low, khatri_high, khatri_low):
    return bf16_dot(high, khatri_high) + (bf16_dot(high, khatri_low) + bf16_dot(low, khatri_high))


def gram_of(high, low):
    t = lambda a, b: lax.dot_general(a, b, (((0,), (0,)), ((), ())), preferred_element_type=F32)
    cross = t(high, low)
    return t(high, high) + (cross + cross.T)


def half_of(ref, core):
    rows = ref.shape[0] // 2
    return ref[pl.ds(pl.multiple_of(core * rows, rows), rows), :]


def piece_kernel(high_ref, low_ref, khatri_ref, *refs):
    so_far, (total_ref, gram_ref) = refs[:-2], refs[-2:]
    _, core = position()
    khatri = halves(khatri_ref[...])
    total = three_dots(half_of(high_ref, 1 - core), half_of(low_ref, 1 - core), *khatri)
    gram = gram_of(*khatri)
    total_ref[...] = total + so_far[0][...] if so_far else total
    gram_ref[...] = gram + so_far[1][...] if so_far else gram


def by_quarters(out_ref, total):
    for place in range(4):
        out_ref[place, :BLOCK, :] = total[place * BLOCK : (place + 1) * BLOCK]


def given_kernel(high_ref, low_ref, khatri_ref, total_ref, gram_ref, out_ref):
    _, core = position()
    khatri = halves(khatri_ref[...])
    by_quarters(out_ref, three_dots(half_of(high_ref, 1 - core), half_of(low_ref, 1 - core), *khatri) + total_ref[...])
    gram = gram_of(*khatri) + gram_ref[...]
    h = gram.shape[0] // 2
    rows, few = h // 4, h // 8
    for place in range(4):
        at, low = slice(place * rows, (place + 1) * rows), place * few
        out_ref[place, BLOCK : BLOCK + rows, :h] = gram[at, :h]
        out_ref[place, BLOCK : BLOCK + rows, h:] = gram[h:, h:][at]
        out_ref[place, BLOCK + rows :, :h] = gram[low : low + few, h:]
        out_ref[place, BLOCK + rows :, h:] = gram[h // 2 + low : h // 2 + low + few, h:]


def kept_kernel(*refs):
    parts, pieces, (given_ref, out_ref) = refs[:8], refs[8:12], refs[12:]
    _, core = position()
    total = None
    for n, khatri_ref in enumerate(pieces):
        part = three_dots(half_of(parts[2 * n], core), half_of(parts[2 * n + 1], core), *halves(khatri_ref[...]))
        total = part if total is None else total + part
    by_quarters(out_ref, total)
    out_ref[:, BLOCK:, :] = given_ref[:, BLOCK:, :]


def pair_kernel(kept_ref, given_ref, *outs):
    z, _ = position()
    for step, out_ref in enumerate(outs):
        place = quarter(z, step)
        out_ref[...] = kept_ref[place] + given_ref[place]


def quarter_kernel(a, b, c, d, product_ref, gram_ref):
    total = (a[...] + b[...]) + (c[...] + d[...])
    product_ref[...] = total[:BLOCK]
    gram_ref[...] = total[BLOCK:]


def from_z(own):
    got = {step: lax.ppermute(own, "samp", along_z(step)) for step in FAR_FIRST}
    return [own, got[1], got[2], got[3]]


def sums_over_row_group(fibres, block, aside):
    rank = block.shape[1]
    rows, samples = fibres.shape
    depth = samples // 4
    flops = 6 * rows * depth * rank
    near = {step: lax.ppermute(block, "row", in_plane(step, 2 * step)) for step in FAR_FIRST}
    piece = joined([block, near[1], near[2], near[3]], lambda: place_in_row()[1])
    fibres, piece = lax.optimization_barrier((fibres, piece))
    parts = split(fibres)
    moves = {-1: (0, 1), 1: (0, -1), 2: (1, 0)}
    pieces = {beside: lax.ppermute(piece, "row", in_plane(*move)) for beside, move in moves.items()}
    pieces[0] = piece
    state = ()
    for n, beside in enumerate(LINES[:3]):
        high, low = parts[2 * n : 2 * n + 2]
        out = (shape(rows // 2, rank), shape(rank, rank))
        state = call(piece_kernel, out, high, low, pieces[beside], *state, flops=flops // 2, size=2**21)
        if n == 0:
            state, extra = lax.optimization_barrier((state, aside(piece)))
    total, gram = state
    high, low = parts[6:]
    out = shape(4, BLOCK + 3 * rank // 16, rank)
    given = call(given_kernel, out, high, low, pieces[2], total, gram, flops=flops, size=2**21)
    got = lax.ppermute(given, "samp", CORE)
    kept = call(kept_kernel, out, *parts, *[pieces[beside] for beside in LINES], given, flops=2 * flops, size=2**23)
    return kept, got, extra


def summed(fibres, block, aside):
    rank = block.shape[1]
    kept, got, extra = sums_over_row_group(fibres, block, aside)
    pairs = call(pair_kernel, (shape(*kept.shape[1:]),) * 4, kept, got, size=2**21)
    parts = [pairs[0]] + [lax.ppermute(pairs[step], "samp", along_z(step)) for step in FAR_FIRST]
    product, gram = call(quarter_kernel, (shape(BLOCK, rank), shape(3 * rank // 16, rank)), *parts, size=2**20)
    h = rank // 2
    first = call(
        first_inverse_kernel,
        (shape(h, h),) * 3,
        *from_z(gram),
        scratch_shapes=[pltpu.VMEM((h, h), F32)] * 3,
        flops=10**11,
        size=2**19,
    )
    first, pieces = lax.optimization_barrier((first, from_z(product)))
    mine = joined(pieces, lambda: position()[0])
    other = lax.ppermute(mine, "samp", CORE)
    inverse = call(second_inverse_kernel, shape(rank, rank), *first, flops=10**11, size=2**19)
    return mine, other, inverse, extra


def solve_into(out_ref, mine_ref, other_ref, inverse_ref):
    _, core = position()
    inverse = halves(inverse_ref[...])
    rows = mine_ref.shape[0]
    for owner, ref in ((core, mine_ref), (1 - core, other_ref)):
        out_ref[pl.ds(pl.multiple_of(owner * rows, rows), rows), :] = three_dots(*halves(ref[...]), *inverse)


def select_kernel(index_ref, c_ref, out_ref, slots_ref):
    select_into(out_ref, 0, slots_of(index_ref, 1, c_ref.shape[0]), c_ref[...])
    slots_ref[...] = slots_of(index_ref, 0, c_ref.shape[0])


def first_solve_kernel(mine_ref, other_ref, inverse_ref, chosen_ref, slots_ref, solved_ref, out_ref):
    solve_into(solved_ref, mine_ref, other_ref, inverse_ref)
    solved = solved_ref[...]
    peers, _, rank = out_ref.shape
    squares = jnp.sum(solved * solved, axis=0, keepdims=True)
    out_ref[:, 2 * CAP :, :] = jnp.broadcast_to(squares[None], (peers, 8, rank))
    out_ref[:, CAP : 2 * CAP, :] = chosen_ref[...]
    select_into(out_ref, 0, slots_ref[...], solved)


def second_solve_kernel(mine_ref, other_ref, inverse_ref, solved_ref, out_ref):
    solve_into(solved_ref, mine_ref, other_ref, inverse_ref)
    solved = solved_ref[...]
    out_ref[...] = jnp.broadcast_to(jnp.sum(solved * solved, axis=0, keepdims=True)[None], out_ref.shape)


def finish_kernel(solved_ref, got_ref, out_ref, scale_ref):
    scale = column_scale(got_ref, 0, solved_ref.shape[0] * got_ref.shape[0])
    scale_ref[...] = scale
    out_ref[...] = solved_ref[...] * (1.0 / scale)


def exchange(rows):
    return lax.all_to_all(rows, "row", 0, 0, tiled=True)


def shards(fibres_first, fibres_second, index_first, index_second, factor_b, factor_c):
    height, rank = factor_b.shape
    peers = index_first.shape[0] // BLOCK
    first, second = index_first.T, index_second.T

    sent, first = first_select(first, factor_b, factor_c)
    got = exchange(sent)
    block = call(lambda *refs: first_khatri_kernel(height, *refs), shape(BLOCK, rank), first, got, flops=10**8, size=2**22)

    def choose(piece):
        index, rows, _ = lax.optimization_barrier((second, factor_c, piece))
        out = (shape(peers, CAP, rank), shape(peers * CAP, height, dtype=BF16))
        return call(select_kernel, out, index, rows, flops=10**9, size=2**21)

    mine, other, inverse, chosen = summed(fibres_first, block, choose)
    solved, sent = call(
        first_solve_kernel,
        (shape(height, rank), shape(peers, 2 * CAP + 8, rank)),
        mine,
        other,
        inverse,
        *chosen,
        flops=10**9,
        size=2**21,
    )
    block, scale = call(
        lambda *refs: second_khatri_kernel(height, *refs),
        (shape(BLOCK, rank), shape(8, rank)),
        second,
        exchange(sent),
        flops=10**8,
        size=2**22,
    )

    def normalise(piece):
        rows, _ = lax.optimization_barrier((solved, piece))
        return rows / scale[:1]

    mine, other, inverse, factor_a = summed(fibres_second, block, normalise)
    solved, sent = call(
        second_solve_kernel,
        (shape(height, rank), shape(peers, 1, rank)),
        mine,
        other,
        inverse,
        flops=10**9,
        size=2**21,
    )
    factor_b_new, weights = call(finish_kernel, (shape(height, rank), shape(1, rank)), solved, exchange(sent), size=2**21)
    return (factor_a, factor_b_new, weights.reshape(rank))


def solution(mesh):
    placed = (P("row", "samp"), P("row", "samp"), P("samp", None), P("samp", None), P("row", None), P("row", None))
    return jax.shard_map(
        shards,
        mesh=mesh,
        in_specs=placed,
        out_specs=(P("row", None), P("row", None), P()),
        check_vma=False,
    )
```
